32 devices in a mesh: dp: 16 (over z, y, x), tensor: 2 (over core).
Axes of the slice: x: 2, y: 2, z: 4, core: 2. Of those that a mesh axis runs over, the one named last changes fastest.
Arguments:
- tokens: bfloat16 [12288, 2048], P(('dp', 'tensor')), may hold values from -6 to 6
- cotangent: bfloat16 [12288, 2048], P(('dp', 'tensor')), may hold values from -6 to 6
- segments: int32 [16, 768], P('dp'), may hold values from 0 to 3, never falling along the last dimension, each value on 1 to 576 neighbouring positions
- query_weight: float32 [2048, 2048], P('dp', 'tensor'), may hold values from -0.125 to 0.125
- key_weight: float32 [2048, 256], P('dp', 'tensor'), may hold values from -0.125 to 0.125
- value_weight: float32 [2048, 256], P('dp', 'tensor'), may hold values from -0.125 to 0.125
- out_weight: float32 [2048, 2048], P('dp', 'tensor'), may hold values from -1 to 1
- gate_weight: float32 [2048, 5632], P('dp', 'tensor'), may hold values from -0.125 to 0.125
- up_weight: float32 [2048, 5632], P('dp', 'tensor'), may hold values from -0.125 to 0.125
- down_weight: float32 [2048, 5632], P('dp', 'tensor'), may hold values from -0.078125 to 0.078125
- norm_gains: float32 [2, 2048], P(None, 'dp'), may hold values from 0.5 to 1.5
- query_moment: float32 [2048, 2048], P('dp', 'tensor'), may hold values from -56 to 56
- key_moment: float32 [2048, 256], P('dp', 'tensor'), may hold values from -160 to 160
- value_moment: float32 [2048, 256], P('dp', 'tensor'), may hold values from -160 to 160
- out_moment: float32 [2048, 2048], P('dp', 'tensor'), may hold values from -10 to 10
- gate_moment: float32 [2048, 5632], P('dp', 'tensor'), may hold values from -20 to 20
- up_moment: float32 [2048, 5632], P('dp', 'tensor'), may hold values from -28 to 28
- down_moment: float32 [2048, 5632], P('dp', 'tensor'), may hold values from -40 to 40
- gains_moment: float32 [2, 2048], P(None, 'dp'), may hold values from -64 to 64
- query_square: float32 [2048, 2048], P('dp', 'tensor'), may hold values from 203.9808 to 1646.592
- key_square: float32 [2048, 256], P('dp', 'tensor'), may hold values from 1695.744 to 13639.68
- value_square: float32 [2048, 256], P('dp', 'tensor'), may hold values from 1695.744 to 13639.68
- out_square: float32 [2048, 2048], P('dp', 'tensor'), may hold values from 7.24992 to 57.7536
- gate_square: float32 [2048, 5632], P('dp', 'tensor'), may hold values from 28.2624 to 233.472
- up_square: float32 [2048, 5632], P('dp', 'tensor'), may hold values from 41.7792 to 331.776
- down_square: float32 [2048, 5632], P('dp', 'tensor'), may hold values from 115.5072 to 933.888
- gains_square: float32 [2, 2048], P(None, 'dp'), may hold values from 319.488 to 2580.48
Outputs:
- activations: bfloat16 [12288, 2048], P(('dp', 'tensor'))
- input_grad: float32 [12288, 2048], P(('dp', 'tensor'))
- query_grad: float32 [2048, 2048], P('dp', 'tensor')
- query_moment_new: float32 [2048, 2048], P('dp', 'tensor')
- query_square_new: float32 [2048, 2048], P('dp', 'tensor')
- query_new: float32 [2048, 2048], P('dp', 'tensor')
- key_grad: float32 [2048, 256], P('dp', 'tensor')
- key_moment_new: float32 [2048, 256], P('dp', 'tensor')
- key_square_new: float32 [2048, 256], P('dp', 'tensor')
- key_new: float32 [2048, 256], P('dp', 'tensor')
- value_grad: float32 [2048, 256], P('dp', 'tensor')
- value_moment_new: float32 [2048, 256], P('dp', 'tensor')
- value_square_new: float32 [2048, 256], P('dp', 'tensor')
- value_new: float32 [2048, 256], P('dp', 'tensor')
- out_grad: float32 [2048, 2048], P('dp', 'tensor')
- out_moment_new: float32 [2048, 2048], P('dp', 'tensor')
- out_square_new: float32 [2048, 2048], P('dp', 'tensor')
- out_new: float32 [2048, 2048], P('dp', 'tensor')
- gate_grad: float32 [2048, 5632], P('dp', 'tensor')
- gate_moment_new: float32 [2048, 5632], P('dp', 'tensor')
- gate_square_new: float32 [2048, 5632], P('dp', 'tensor')
- gate_new: float32 [2048, 5632], P('dp', 'tensor')
- up_grad: float32 [2048, 5632], P('dp', 'tensor')
- up_moment_new: float32 [2048, 5632], P('dp', 'tensor')
- up_square_new: float32 [2048, 5632], P('dp', 'tensor')
- up_new: float32 [2048, 5632], P('dp', 'tensor')
- down_grad: float32 [2048, 5632], P('dp', 'tensor')
- down_moment_new: float32 [2048, 5632], P('dp', 'tensor')
- down_square_new: float32 [2048, 5632], P('dp', 'tensor')
- down_new: float32 [2048, 5632], P('dp', 'tensor')
- gains_grad: float32 [2, 2048], P(None, 'dp')
- gains_moment_new: float32 [2, 2048], P(None, 'dp')
- gains_square_new: float32 [2, 2048], P(None, 'dp')
- gains_new: float32 [2, 2048], P(None, 'dp')
The draws below stay inside these ranges and needn't reach their ends.
Inputs may be any that keep to these rules, and one draw needn't show every extreme that they name: `segments`: within each sequence the numbers never fall, each number marks one document of at most 576 tokens, and one document of every sequence has exactly 576 tokens.
All inputs are finite; a program needn't handle non-finite values.
Results may differ from the reference program's by a relative error of at most 0.014.
The reference program's roundings to bfloat16 on the way count: a program that leaves them out, or rounds other values in their place, can miss the bound.
Values may be sent and summed in bfloat16 or wider, within the bound.
No kernel may reach another device: no remote copies, remote signals or barrier semaphores. Data moves between devices by JAX's collectives and lax.ppermute only.
A program may use at most 320 MiB of HBM per device.

```python
import math
import jax
import jax.numpy as jnp
import numpy as np
from jax import lax

D = 2048
HEADS = 32
KV_HEADS = 4
HEAD = 64
FF = 5632
SEQ_LEN = 768
DOCS = 4
STEP = 10
DOC_MOST = 576
QW = 2048
KVW = 256
SEQS = 16
TOKENS = 12288


def steps_of(stream_key, shape, split, low, largest):
    loudness, own = 1.0, jax.random.fold_in(stream_key, 6)
    for axis_at, shards_of in split:
        heights = jnp.exp(jax.random.uniform(jax.random.fold_in(own, axis_at), (shards_of,), jnp.float32, low / len(split), largest / len(split)))
        loudness = loudness * jnp.repeat(heights, shape[axis_at] // shards_of).reshape([-1 if axis == axis_at else 1 for axis in range(len(shape))])
    return loudness


def profile(amount, total, limit, skew):
    portions = [(1 << 20) // math.isqrt(standing ** skew) + 1 for standing in range(2, amount + 1)]
    spare, holding = total - limit - (amount - 1), [1] * (amount - 1)
    while spare > 0:
        candidates = [i for i in range(amount - 1) if holding[i] < limit]
        whole, remaining = sum([portions[i] for i in candidates]), spare
        for i in candidates:
            extra = min(limit - holding[i], max(1, remaining * portions[i] // whole), spare)
            holding[i] = holding[i] + extra
            spare = spare - extra
    return np.array([limit] + holding)


def uneven(key, amount, total, most, lean):
    if amount == 2:
        one = jax.random.randint(key, (), max(1, total - most), min(most, total - 1) + 1)
        return jnp.stack([one, total - one])
    sizes = jnp.asarray(profile(amount, total, most, lean), jnp.int32)
    couples = (amount - 1) // 2
    source_of, sink = sizes[1:1 + 2 * couples:2], sizes[2:2 + 2 * couples:2]
    slack = jnp.minimum(source_of - 1, most - sink)
    shifted = jax.random.randint(jax.random.fold_in(key, 1), (couples,), 0, 1 << 20) % (slack + 1)
    sizes = sizes.at[1:1 + 2 * couples:2].set(source_of - shifted).at[2:2 + 2 * couples:2].set(sink + shifted)
    return sizes[jax.random.permutation(jax.random.fold_in(key, 2), amount)]


def noise(key, dims, spread, most, shards=(), held_as=jnp.bfloat16):
    values = spread * jax.random.normal(key, dims, jnp.float32)
    if shards:
        values = values * steps_of(key, dims, shards, -0.22, 0.18)
    return jnp.clip(values, -most, most).astype(held_as)


def setup_inputs(seed: int = 0) -> dict:
    key_of = jax.random.split(jax.random.key(seed), 28)
    tokens = noise(key_of[0], (TOKENS, D), 1.0, 6.0, ((0, 32),))
    cotangent = noise(key_of[1], (TOKENS, D), 1.0, 6.0, ((0, 32),))
    segments = jax.vmap(lambda own: jnp.searchsorted(jnp.cumsum(uneven(own, DOCS, SEQ_LEN, DOC_MOST, 0)), jnp.arange(SEQ_LEN), side="right"))(jax.random.split(key_of[2], SEQS)).reshape((SEQS, SEQ_LEN)).astype(jnp.int32)
    query_weight = noise(key_of[3], (D, QW), D ** -0.5, 0.125, ((0, 16), (1, 2)), jnp.float32)
    key_weight = noise(key_of[4], (D, KVW), D ** -0.5, 0.125, ((0, 16), (1, 2)), jnp.float32)
    value_weight = noise(key_of[5], (D, KVW), D ** -0.5, 0.125, ((0, 16), (1, 2)), jnp.float32)
    out_weight = noise(key_of[6], (D, QW), 32 ** -0.5, 1.0, ((0, 16), (1, 2)), jnp.float32)
    gate_weight = noise(key_of[7], (D, FF), D ** -0.5, 0.125, ((0, 16), (1, 2)), jnp.float32)
    up_weight = noise(key_of[8], (D, FF), D ** -0.5, 0.125, ((0, 16), (1, 2)), jnp.float32)
    down_weight = noise(key_of[9], (D, FF), FF ** -0.5, 0.078125, ((0, 16), (1, 2)), jnp.float32)
    norm_gains = jnp.clip(1.0 + 0.1 * jax.random.normal(key_of[10], (2, D), jnp.float32), 0.5, 1.5)
    query_moment = noise(key_of[11], (D, QW), (0.088 * TOKENS ** 0.5), 56.0, ((0, 16), (1, 2)), jnp.float32)
    key_moment = noise(key_of[12], (D, KVW), (0.25 * TOKENS ** 0.5), 160.0, ((0, 16), (1, 2)), jnp.float32)
    value_moment = noise(key_of[13], (D, KVW), (0.25 * TOKENS ** 0.5), 160.0, ((0, 16), (1, 2)), jnp.float32)
    out_moment = noise(key_of[14], (D, QW), (0.0165 * TOKENS ** 0.5), 10.0, ((0, 16), (1, 2)), jnp.float32)
    gate_moment = noise(key_of[15], (D, FF), (0.033 * TOKENS ** 0.5), 20.0, ((0, 16), (1, 2)), jnp.float32)
    up_moment = noise(key_of[16], (D, FF), (0.04 * TOKENS ** 0.5), 28.0, ((0, 16), (1, 2)), jnp.float32)
    down_moment = noise(key_of[17], (D, FF), (0.066 * TOKENS ** 0.5), 40.0, ((0, 16), (1, 2)), jnp.float32)
    gains_moment = noise(key_of[18], (2, D), (0.11 * TOKENS ** 0.5), 64.0, ((1, 16),), jnp.float32)
    query_square = jnp.clip(jnp.exp(math.log(1646.592) - 2.088437 * jax.random.uniform(key_of[19], (D, QW), jnp.float32) ** steps_of(key_of[19], (D, QW), ((0, 16), (1, 2)), -0.2, 0.2)), 203.9808, 1646.592)
    key_square = jnp.clip(jnp.exp(math.log(13639.68) - 2.0848616 * jax.random.uniform(key_of[20], (D, KVW), jnp.float32) ** steps_of(key_of[20], (D, KVW), ((0, 16), (1, 2)), -0.2, 0.2)), 1695.744, 13639.68)
    value_square = jnp.clip(jnp.exp(math.log(13639.68) - 2.0848616 * jax.random.uniform(key_of[21], (D, KVW), jnp.float32) ** steps_of(key_of[21], (D, KVW), ((0, 16), (1, 2)), -0.2, 0.2)), 1695.744, 13639.68)
    out_square = jnp.clip(jnp.exp(math.log(57.7536) - 2.0751953 * jax.random.uniform(key_of[22], (D, QW), jnp.float32) ** steps_of(key_of[22], (D, QW), ((0, 16), (1, 2)), -0.2, 0.2)), 7.24992, 57.7536)
    gate_square = jnp.clip(jnp.exp(math.log(233.472) - 2.1115299 * jax.random.uniform(key_of[23], (D, FF), jnp.float32) ** steps_of(key_of[23], (D, FF), ((0, 16), (1, 2)), -0.2, 0.2)), 28.2624, 233.472)
    up_square = jnp.clip(jnp.exp(math.log(331.776) - 2.0720614 * jax.random.uniform(key_of[24], (D, FF), jnp.float32) ** steps_of(key_of[24], (D, FF), ((0, 16), (1, 2)), -0.2, 0.2)), 41.7792, 331.776)
    down_square = jnp.clip(jnp.exp(math.log(933.888) - 2.0900236 * jax.random.uniform(key_of[25], (D, FF), jnp.float32) ** steps_of(key_of[25], (D, FF), ((0, 16), (1, 2)), -0.2, 0.2)), 115.5072, 933.888)
    gains_square = jnp.clip(jnp.exp(math.log(2580.48) - 2.089011 * jax.random.uniform(key_of[26], (2, D), jnp.float32) ** steps_of(key_of[26], (2, D), ((1, 16),), -0.2, 0.2)), 319.488, 2580.48)
    return dict(tokens=tokens, cotangent=cotangent, segments=segments, query_weight=query_weight, key_weight=key_weight, value_weight=value_weight, out_weight=out_weight, gate_weight=gate_weight, up_weight=up_weight, down_weight=down_weight, norm_gains=norm_gains, query_moment=query_moment, key_moment=key_moment, value_moment=value_moment, out_moment=out_moment, gate_moment=gate_moment, up_moment=up_moment, down_moment=down_moment, gains_moment=gains_moment, query_square=query_square, key_square=key_square, value_square=value_square, out_square=out_square, gate_square=gate_square, up_square=up_square, down_square=down_square, gains_square=gains_square)


NORM_EPS = 1e-05
NEG_LARGE = -1000000000.0
BETA_FIRST = 0.9
BETA_SECOND = 0.95
ADAM_EPS = 1e-08
DECAY_RATE = 0.1
RATE_MAIN = 0.02
RATE_OUT = 0.15
RATE_DOWN = 0.015
RATE_GAINS = 0.6
HIGHEST = lax.Precision.HIGHEST

@jax.custom_vjp
def low(v):
    return lax.optimization_barrier(v.astype(jnp.bfloat16)).astype(jnp.float32)

@jax.custom_vjp
def low_back(v):
    return v

def low_keep(v):
    return (low(v), None)

def low_pass(kept, grad):
    return (grad,)

def back_keep(v):
    return (v, None)

def back_low(kept, grad):
    return (low(grad),)
low.defvjp(low_keep, low_pass)
low_back.defvjp(back_keep, back_low)

def rope_tables(segment):
    length = segment.shape[0]
    order = jnp.arange(length, dtype=jnp.int32)
    before = lax.optimization_barrier(jnp.sum((segment[None, :] < segment[:, None]).astype(jnp.int32), axis=1))
    place = (order - before).astype(jnp.float32)
    half = HEAD // 2
    freq = jnp.exp(jnp.arange(half, dtype=jnp.float32) * (-2.0 * math.log(10000.0) / HEAD))
    angle = place[:, None] * freq[None, :]
    return (jnp.cos(angle)[:, None, :], jnp.sin(angle)[:, None, :])

def allowed_pairs(segment):
    length = segment.shape[0]
    order = jnp.arange(length, dtype=jnp.int32)
    return (segment[:, None] == segment[None, :]) & (order[None, :] <= order[:, None])

def rotate(values, cosine, sine):
    half = HEAD // 2
    first = values[..., :half]
    second = values[..., half:]
    return jnp.concatenate([first * cosine - second * sine, second * cosine + first * sine], axis=-1)

def norm(values, gain):
    return values * lax.rsqrt(lax.optimization_barrier(jnp.mean(values * values, axis=-1, keepdims=True)) + NORM_EPS) * gain

def matmul(left, right):
    return jnp.dot(left, right, precision=HIGHEST)

def layer(inputs, query_w, key_w, value_w, out_w, gate_w, up_w, down_w, gains, segment):
    length = inputs.shape[0]
    ratio = HEADS // KV_HEADS
    gain_low = low(gains)
    cosine, sine = rope_tables(segment)
    allowed = allowed_pairs(segment)
    normed_one = low(norm(inputs, gain_low[0]))
    query_pre = low_back(matmul(normed_one, low(query_w)))
    key_pre = low_back(matmul(normed_one, low(key_w)))
    value_pre = low_back(matmul(normed_one, low(value_w)))
    queries = low(rotate(query_pre.reshape(length, HEADS, HEAD), cosine, sine)).reshape(length, KV_HEADS, ratio, HEAD)
    keys = low(rotate(key_pre.reshape(length, KV_HEADS, HEAD), cosine, sine))
    values = low(value_pre).reshape(length, KV_HEADS, HEAD)
    raw = low_back(jnp.einsum('qgrd,kgd->grqk', queries, keys, precision=HIGHEST))
    score = jnp.where(allowed[None, None], raw * HEAD ** (-0.5), NEG_LARGE)
    probs = low(jax.nn.softmax(score, axis=-1))
    attended = jnp.einsum('grqk,kgd->qgrd', probs, values, precision=HIGHEST).reshape(length, HEADS * HEAD)
    attended = low(low_back(attended))
    hidden_state = inputs + low_back(matmul(attended, low(out_w).T))
    normed_two = low(norm(hidden_state, gain_low[1]))
    gate = low_back(matmul(normed_two, low(gate_w)))
    upper = low_back(matmul(normed_two, low(up_w)))
    inner = low(jax.nn.silu(gate) * upper)
    return hidden_state + low_back(matmul(inner, low(down_w).T))

def adam(weight, grad, moment, square, rate, decay):
    moment_new = BETA_FIRST * moment + (1.0 - BETA_FIRST) * grad
    square_new = BETA_SECOND * square + (1.0 - BETA_SECOND) * grad * grad
    direction = moment_new / (1.0 - BETA_FIRST ** STEP) / (jnp.sqrt(square_new / (1.0 - BETA_SECOND ** STEP)) + ADAM_EPS)
    return (grad, moment_new, square_new, weight - rate * (direction + decay * weight))

def reference(tokens, cotangent, segments, query_weight, key_weight, value_weight, out_weight, gate_weight, up_weight, down_weight, norm_gains, query_moment, key_moment, value_moment, out_moment, gate_moment, up_moment, down_moment, gains_moment, query_square, key_square, value_square, out_square, gate_square, up_square, down_square, gains_square):
    weights = (query_weight, key_weight, value_weight, out_weight, gate_weight, up_weight, down_weight, norm_gains)

    def per_sequence(carry, item):
        inputs, upstream, segment = item

        def forward(block_in, *params):
            return layer(block_in, *params, segment)
        result, pullback = jax.vjp(forward, inputs.astype(jnp.float32), *weights)
        grads = pullback(upstream.astype(jnp.float32))
        summed = tuple((total + piece for total, piece in zip(carry, grads[1:])))
        return (summed, (result.astype(jnp.bfloat16), grads[0]))
    init = tuple((jnp.zeros(w.shape, jnp.float32) for w in weights))
    sums, (outs, input_grads) = lax.scan(per_sequence, init, (tokens.reshape(SEQS, SEQ_LEN, D), cotangent.reshape(SEQS, SEQ_LEN, D), segments))
    q_all = adam(query_weight, sums[0], query_moment, query_square, RATE_MAIN, DECAY_RATE)
    k_all = adam(key_weight, sums[1], key_moment, key_square, RATE_MAIN, DECAY_RATE)
    v_all = adam(value_weight, sums[2], value_moment, value_square, RATE_MAIN, DECAY_RATE)
    o_all = adam(out_weight, sums[3], out_moment, out_square, RATE_OUT, DECAY_RATE)
    g_all = adam(gate_weight, sums[4], gate_moment, gate_square, RATE_MAIN, DECAY_RATE)
    u_all = adam(up_weight, sums[5], up_moment, up_square, RATE_MAIN, DECAY_RATE)
    d_all = adam(down_weight, sums[6], down_moment, down_square, RATE_DOWN, DECAY_RATE)
    n_all = adam(norm_gains, sums[7], gains_moment, gains_square, RATE_GAINS, 0.0)
    return (outs.reshape(TOKENS, D), input_grads.reshape(TOKENS, D), q_all[0], q_all[1], q_all[2], q_all[3], k_all[0], k_all[1], k_all[2], k_all[3], v_all[0], v_all[1], v_all[2], v_all[3], o_all[0], o_all[1], o_all[2], o_all[3], g_all[0], g_all[1], g_all[2], g_all[3], u_all[0], u_all[1], u_all[2], u_all[3], d_all[0], d_all[1], d_all[2], d_all[3], n_all[0], n_all[1], n_all[2], n_all[3])
```

```python
import functools
import math

import jax
import jax.numpy as jnp
from jax import lax
from jax.experimental import pallas as pl
from jax.experimental.pallas import tpu as pltpu
from jax.sharding import PartitionSpec as P

HEAD = 64
STEP = 10


NORM_EPS = 1e-05
NEG_LARGE = -1000000000.0
BETA_FIRST = 0.9
BETA_SECOND = 0.95
ADAM_EPS = 1e-08
DECAY_RATE = 0.1
RATE_MAIN = 0.02
RATE_OUT = 0.15
RATE_DOWN = 0.015
RATE_GAINS = 0.6


def rope_tables(segment):
    length = segment.shape[0]
    order = jnp.arange(length, dtype=jnp.int32)
    before = jnp.sum((segment[None, :] < segment[:, None]).astype(jnp.int32), axis=1)
    place = (order - before).astype(jnp.float32)
    half = HEAD // 2
    freq = jnp.exp(jnp.arange(half, dtype=jnp.float32) * (-2.0 * math.log(10000.0) / HEAD))
    angle = place[:, None] * freq[None, :]
    cosine, sine = jnp.cos(angle), jnp.sin(angle)
    return (
        jnp.concatenate([cosine] * 4, axis=1),
        jnp.concatenate([-sine, sine, -sine, sine], axis=1),
    )


def norm_back(values, inverse, gain, upstream):
    weighted = gain * upstream
    grad_in = inverse * weighted - values * inverse**3 * jnp.mean(
        weighted * values, axis=1, keepdims=True
    )
    grad_gain = jnp.sum(upstream * values * inverse, axis=0)
    return (grad_in, grad_gain)


def contract_rows(left, right):
    return lax.dot_general(
        left, right, (((0,), (0,)), ((), ())), preferred_element_type=jnp.float32
    )


def contract_cols(left, right):
    return lax.dot_general(
        left, right, (((1,), (1,)), ((), ())), preferred_element_type=jnp.float32
    )


def adam(weight, grad, moment, square, rate, decay):
    moment_new = BETA_FIRST * moment + (1.0 - BETA_FIRST) * grad
    square_new = BETA_SECOND * square + (1.0 - BETA_SECOND) * grad * grad
    direction = (
        moment_new
        / (1.0 - BETA_FIRST**STEP)
        / (jnp.sqrt(square_new / (1.0 - BETA_SECOND**STEP)) + ADAM_EPS)
    )
    return (grad, moment_new, square_new, weight - rate * (direction + decay * weight))


LOW = jnp.bfloat16
PLANE = 4
LANES = 128
TILE = 256
VMEM_LIMIT = 48 * 1024 * 1024


def swap_cores(block):
    return lax.ppermute(block, "tensor", [(0, 1), (1, 0)])


def lane_of(shape):
    return lax.broadcasted_iota(jnp.int32, shape, len(shape) - 1)


def turn_heads(values, cosine, sine):
    first = lane_of(values.shape) % HEAD < HEAD // 2
    ahead = pltpu.roll(values, LANES - HEAD // 2, 1)
    behind = pltpu.roll(values, HEAD // 2, 1)
    return values * cosine + jnp.where(first, ahead, behind) * sine


def project_kernel(heads, normed_ref, weight_ref, cosine_ref, sine_ref, out_ref):
    part = jnp.dot(normed_ref[...], weight_ref[...], preferred_element_type=jnp.float32)
    cosine, sine = cosine_ref[...], sine_ref[...]
    step = pl.program_id(0)
    for at in range(0, part.shape[1], LANES):
        piece = part[:, at : at + LANES]
        turned = turn_heads(piece, cosine, sine)
        keep = step * part.shape[1] + at >= heads
        out_ref[:, at : at + LANES] = jnp.where(keep, piece, turned).astype(LOW)


def project(normed, weight, cosine, sine, turned):
    rows, depth = normed.shape
    columns = weight.shape[1]
    block = 2 * LANES
    return pl.pallas_call(
        functools.partial(project_kernel, turned),
        grid=(columns // block,),
        in_specs=[
            pl.BlockSpec((rows, depth), lambda i: (0, 0)),
            pl.BlockSpec((depth, block), lambda i: (0, i)),
            pl.BlockSpec((rows, LANES), lambda i: (0, 0)),
            pl.BlockSpec((rows, LANES), lambda i: (0, 0)),
        ],
        out_specs=pl.BlockSpec((rows, block), lambda i: (0, i)),
        out_shape=jax.ShapeDtypeStruct((rows, columns), LOW),
        compiler_params=pltpu.CompilerParams(vmem_limit_bytes=VMEM_LIMIT),
        cost_estimate=pl.CostEstimate(
            flops=2 * rows * depth * columns,
            bytes_accessed=2 * (rows * depth + depth * columns + rows * columns),
            transcendentals=0,
        ),
    )(normed, weight, cosine, sine)


def double(values, group):
    low_half = lane_of(values.shape) < HEAD
    other = pltpu.roll(values.astype(jnp.float32), HEAD, 1).astype(values.dtype)
    return jnp.where(low_half == (group == 0), values, other)


def set_bias(across_ref, down_ref, bias):
    rows = bias.shape[0]
    row = lax.broadcasted_iota(jnp.int32, (rows, rows), 0)
    column = lax.broadcasted_iota(jnp.int32, (rows, rows), 1)
    allowed = (down_ref[...] == across_ref[...]) & (column <= row)
    bias[...] = jnp.where(allowed, 0.0, NEG_LARGE)


def halves_of(block):
    low_half = lane_of(block.shape) < HEAD
    zero = jnp.zeros_like(block)
    return jnp.where(low_half, block, zero), jnp.where(low_half, zero, block)


def dot_last(left, right):
    return lax.dot_general(
        left, right, (((1,), (1,)), ((), ())), preferred_element_type=jnp.float32
    )


def dot_first(left, right):
    return lax.dot_general(
        left, right, (((0,), (0,)), ((), ())), preferred_element_type=jnp.float32
    )


def attend_kernel(
    per_group, query_ref, key_ref, value_ref, across_ref, down_ref, out_ref, total_ref, bias, keys, values
):
    step = pl.program_id(0)
    rows = query_ref.shape[0]

    @pl.when(step == 0)
    def _():
        set_bias(across_ref, down_ref, bias)
        total_ref[...] = jnp.zeros_like(total_ref)

    @pl.when(step % per_group == 0)
    def _():
        group = step // per_group
        keys[...] = double(key_ref[...], group)
        values[...] = double(value_ref[...], group)

    for start in range(0, rows, TILE):
        stop = start + TILE
        query = query_ref[start:stop, :] * jnp.asarray(HEAD**-0.5, LOW)
        key, value = keys[:stop, :], values[:stop, :]
        shade = bias[start:stop, :stop]
        outs = []
        lane = lane_of((TILE, LANES))
        totals = total_ref[start:stop, :]
        for side, part in enumerate(halves_of(query)):
            score = dot_last(part, key) + shade
            largest = jnp.max(score, axis=1, keepdims=True)
            expo = jnp.exp(score - largest)
            total = jnp.sum(expo, axis=1, keepdims=True)
            probs = (expo * (1.0 / total)).astype(LOW)
            outs.append(jnp.dot(probs, value, preferred_element_type=jnp.float32))
            totals = jnp.where(lane == 2 * step + side, largest + jnp.log(total), totals)
        total_ref[start:stop, :] = totals
        out_ref[start:stop, :] = jnp.where(lane < HEAD, outs[0], outs[1]).astype(LOW)


def attend(into, segment, query_cols):
    rows = into.shape[0]
    pairs = query_cols // LANES
    return pl.pallas_call(
        functools.partial(attend_kernel, pairs // 2),
        grid=(pairs,),
        in_specs=[
            pl.BlockSpec((rows, LANES), lambda i: (0, i)),
            pl.BlockSpec((rows, LANES), lambda i: (0, pairs)),
            pl.BlockSpec((rows, LANES), lambda i: (0, pairs + 1)),
            pl.BlockSpec((1, rows), lambda i: (0, 0)),
            pl.BlockSpec((rows, 1), lambda i: (0, 0)),
        ],
        out_specs=[
            pl.BlockSpec((rows, LANES), lambda i: (0, i)),
            pl.BlockSpec((rows, LANES), lambda i: (0, 0)),
        ],
        out_shape=[
            jax.ShapeDtypeStruct((rows, query_cols), LOW),
            jax.ShapeDtypeStruct((rows, LANES), jnp.float32),
        ],
        scratch_shapes=[
            pltpu.VMEM((rows, rows), jnp.float32),
            pltpu.VMEM((rows, LANES), LOW),
            pltpu.VMEM((rows, LANES), LOW),
        ],
        compiler_params=pltpu.CompilerParams(vmem_limit_bytes=VMEM_LIMIT),
        cost_estimate=pl.CostEstimate(
            flops=8 * rows * rows * query_cols,
            bytes_accessed=6 * rows * query_cols,
            transcendentals=rows * rows * query_cols // HEAD,
        ),
    )(into, into, into, segment[None, :], segment[:, None])


def attend_back_kernel(
    per_group,
    query_ref,
    key_ref,
    value_ref,
    upstream_ref,
    total_ref,
    cosine_ref,
    sine_ref,
    across_ref,
    down_ref,
    query_back_ref,
    rest_ref,
    bias,
    keys,
    values,
    key_sum,
    value_sum,
):
    step = pl.program_id(0)
    rows = query_ref.shape[0]
    group = step // per_group

    @pl.when(step == 0)
    def _():
        set_bias(across_ref, down_ref, bias)

    @pl.when(step % per_group == 0)
    def _():
        keys[...] = double(key_ref[...], group)
        values[...] = double(value_ref[...], group)
        key_sum[...] = jnp.zeros_like(key_sum)
        value_sum[...] = jnp.zeros_like(value_sum)

    scale = jnp.asarray(HEAD**-0.5, LOW)
    for start in range(0, rows, TILE):
        stop = start + TILE
        query = query_ref[start:stop, :] * scale
        upstream = upstream_ref[start:stop, :]
        key, value = keys[:stop, :], values[:stop, :]
        shade = bias[start:stop, :stop]
        lane = lane_of((TILE, LANES))
        backs = []
        key_part = value_part = None
        for side, (part, grad) in enumerate(zip(halves_of(query), halves_of(upstream))):
            log_total = jnp.sum(
                jnp.where(lane == 2 * step + side, total_ref[start:stop, :], 0.0),
                axis=1,
                keepdims=True,
            )
            probs = jnp.exp(dot_last(part, key) + shade - log_total)
            value_here = dot_first(probs.astype(LOW), grad)
            probs_grad = dot_last(grad, value)
            delta = jnp.sum(probs * probs_grad, axis=1, keepdims=True)
            score_grad = (probs * (probs_grad - delta)).astype(LOW)
            backs.append(jnp.dot(score_grad, key, preferred_element_type=jnp.float32))
            key_here = dot_first(score_grad, part)
            key_part = key_here if key_part is None else key_part + key_here
            value_part = value_here if value_part is None else value_part + value_here
        key_sum[:stop, :] += key_part
        value_sum[:stop, :] += value_part
        back = jnp.where(lane < HEAD, backs[0], backs[1]) * HEAD**-0.5
        back = turn_heads(back, cosine_ref[start:stop, :], -sine_ref[start:stop, :])
        query_back_ref[start:stop, :] = back.astype(LOW)

    @pl.when(step % per_group == per_group - 1)
    def _():
        key_back = key_sum[...] + pltpu.roll(key_sum[...], HEAD, 1)
        key_back = turn_heads(key_back, cosine_ref[...], -sine_ref[...]).astype(LOW)
        value_back = (value_sum[...] + pltpu.roll(value_sum[...], HEAD, 1)).astype(LOW)

        @pl.when(group == 0)
        def _():
            rest_ref[:, :LANES] = key_back
            rest_ref[:, LANES:] = value_back

        @pl.when(group == 1)
        def _():
            low_half = lane_of(key_back.shape) < HEAD
            rest_ref[:, :LANES] = jnp.where(low_half, rest_ref[:, :LANES], key_back)
            rest_ref[:, LANES:] = jnp.where(low_half, rest_ref[:, LANES:], value_back)


def attend_back(into, upstream, log_totals, cosine, sine, segment):
    rows, query_cols = upstream.shape
    pairs = query_cols // LANES
    whole = lambda width: pl.BlockSpec((rows, width), lambda i: (0, 0))
    return pl.pallas_call(
        functools.partial(attend_back_kernel, pairs // 2),
        grid=(pairs,),
        in_specs=[
            pl.BlockSpec((rows, LANES), lambda i: (0, i)),
            pl.BlockSpec((rows, LANES), lambda i: (0, pairs)),
            pl.BlockSpec((rows, LANES), lambda i: (0, pairs + 1)),
            pl.BlockSpec((rows, LANES), lambda i: (0, i)),
            whole(LANES),
            whole(LANES),
            whole(LANES),
            pl.BlockSpec((1, rows), lambda i: (0, 0)),
            whole(1),
        ],
        out_specs=[pl.BlockSpec((rows, LANES), lambda i: (0, i)), whole(2 * LANES)],
        out_shape=[
            jax.ShapeDtypeStruct((rows, query_cols), LOW),
            jax.ShapeDtypeStruct((rows, 2 * LANES), LOW),
        ],
        scratch_shapes=[
            pltpu.VMEM((rows, rows), jnp.float32),
            pltpu.VMEM((rows, LANES), LOW),
            pltpu.VMEM((rows, LANES), LOW),
            pltpu.VMEM((rows, LANES), jnp.float32),
            pltpu.VMEM((rows, LANES), jnp.float32),
        ],
        compiler_params=pltpu.CompilerParams(vmem_limit_bytes=VMEM_LIMIT),
        cost_estimate=pl.CostEstimate(
            flops=20 * rows * rows * query_cols,
            bytes_accessed=8 * rows * query_cols,
            transcendentals=rows * rows * query_cols // HEAD,
        ),
    )(into, into, into, upstream, log_totals, cosine, sine, segment[None, :], segment[:, None])
def nothing_kernel(*refs):
    del refs


def after(value, *earlier):
    place = pl.BlockSpec(memory_space=pl.ANY)
    return pl.pallas_call(
        nothing_kernel,
        in_specs=[place] * (1 + len(earlier)),
        out_specs=place,
        out_shape=jax.ShapeDtypeStruct(value.shape, value.dtype),
        input_output_aliases={0: 0},
        compiler_params=pltpu.CompilerParams(vmem_limit_bytes=1024 * 1024),
    )(value, *earlier)


def copy_kernel(plan, count, spots_ref, *refs):
    *blocks, sems = refs
    moves = plan(spots_ref, blocks[:count], blocks[count:])
    copies = [
        pltpu.make_async_copy(source, target, sems.at[at])
        for at, (source, target) in enumerate(moves)
    ]
    for copy in copies:
        copy.start()
    for copy in copies:
        copy.wait()


def assemble(plan, moves, spots, blocks, shapes):
    place = pl.BlockSpec(memory_space=pl.ANY)
    return pl.pallas_call(
        functools.partial(copy_kernel, plan, len(blocks)),
        in_specs=[pl.BlockSpec(memory_space=pltpu.SMEM)] + [place] * len(blocks),
        out_specs=[place] * len(shapes),
        out_shape=[jax.ShapeDtypeStruct(shape, LOW) for shape in shapes],
        scratch_shapes=[pltpu.SemaphoreType.DMA((moves,))],
        compiler_params=pltpu.CompilerParams(vmem_limit_bytes=1024 * 1024),
    )(spots, *blocks)


def wide(block):
    return block.astype(jnp.float32)


def low(block):
    return block.astype(LOW)


def order_cores(own, other, axis=0):
    return jnp.where(
        lax.axis_index("tensor") == 0,
        jnp.concatenate([own, other], axis=axis),
        jnp.concatenate([other, own], axis=axis),
    )


class Links:
    def __init__(self, devices):
        self.devices = devices
        self.planes = devices // PLANE
        self.pairs = {
            step: [(index, index ^ step) for index in range(devices)] for step in (1, 2, 3)
        }
        self.columns = [list(range(corner, devices, PLANE)) for corner in range(PLANE)]
        self.ring = [(index, (index + PLANE) % devices) for index in range(devices)]

    def swap(self, block, step):
        return lax.ppermute(block, "dp", self.pairs[step])

    def turn(self, block):
        return lax.ppermute(block, "dp", self.ring)

    def place(self):
        index = lax.axis_index("dp")
        return index // PLANE, index % PLANE

    def plane_gather(self, block):
        half = block.shape[0] // 2
        first = self.swap(block, 1)
        second = self.swap(block, 2)
        far = [self.swap(second[:half], 1), self.swap(first[half:], 2)]
        return [block, first, second, jnp.concatenate(far, axis=0)]

    def plane_sum(self, blocks):
        own, first, second, far = blocks
        half = own.shape[0] // 2
        far_one = self.swap(low(far[:half]), 1)
        far_two = self.swap(low(far[half:]), 2)
        send_one = jnp.concatenate(
            [low(first[:half]), low(wide(first[half:]) + wide(far_two))], axis=0
        )
        send_two = jnp.concatenate(
            [low(wide(second[:half]) + wide(far_one)), low(second[half:])], axis=0
        )
        return wide(own) + wide(self.swap(send_one, 1)) + wide(self.swap(send_two, 2))

    def ring_slots(self, block):
        slots = [block]
        for _ in range(self.planes - 1):
            slots.append(self.turn(slots[-1]))
        return slots

    def ring_sum(self, part_of):
        level, _ = self.place()
        total = part_of((level - 1) % self.planes)
        for step in range(1, self.planes):
            arrived = wide(self.turn(low(total)))
            total = arrived + part_of((level - 1 - step) % self.planes)
        return total

    def gather_rows(self, block, first, begin):
        level, corner = self.place()
        rows, columns = block.shape
        slots = self.ring_slots(block)
        group = max(1, self.planes // 2)
        pieces, spots = [], []
        for start in range(0, self.planes, group):
            bundle = jnp.concatenate(slots[start : start + group], axis=0)
            for other, piece in enumerate(self.plane_gather(after(bundle, begin))):
                pieces.append(piece.reshape(group, rows, columns))
                spots += [
                    ((level - start - step) % self.planes) * PLANE + (corner ^ other)
                    for step in range(group)
                ]
            begin = pieces[-1]

        def plan(spots_ref, sources, targets):
            moves = []
            for at, source in enumerate(sources):
                for step in range(group):
                    spot = spots_ref[at * group + step]
                    moves.append((source.at[step, :, :first], targets[0].at[spot]))
                    moves.append((source.at[step, :, first:], targets[1].at[spot]))
            return moves

        shapes = [(self.devices, rows, first), (self.devices, rows, columns - first)]
        whole = assemble(plan, 2 * len(spots), jnp.stack(spots), pieces, shapes)
        return [part.reshape(-1, part.shape[2]) for part in whole], begin

    def scatter_rows(self, part):
        _, corner = self.place()
        rows, columns = part.shape[0] // self.devices, part.shape[1]
        parts = part.reshape(self.planes, PLANE, rows, columns)
        sums = self.plane_sum(
            [
                lax.dynamic_index_in_dim(parts, corner ^ other, 1, False).reshape(-1, columns)
                for other in range(PLANE)
            ]
        )
        return self.ring_sum(lambda plane: lax.dynamic_slice_in_dim(sums, plane * rows, rows, 0))

    def spread_units(self, weights):
        core = lax.axis_index("tensor")
        _, corner = self.place()
        rows, columns = weights[0].shape
        wanted = columns // 2
        pieces = jnp.stack(
            [
                jnp.concatenate(
                    [low(weight[:, half * wanted : (half + 1) * wanted]) for weight in weights],
                    axis=1,
                )
                for half in range(2)
            ],
            axis=0,
        ).reshape(2, 2, rows // 2, wanted * len(weights))
        keep = lax.dynamic_index_in_dim(pieces, core, 1, False)
        give = lax.dynamic_index_in_dim(pieces, 1 - core, 1, False)
        quarters = order_cores(keep, swap_cores(give))
        arrived = []
        for other in range(PLANE):
            piece = lax.dynamic_slice_in_dim(quarters, corner ^ other, 1, 0)
            arrived.append(self.swap(piece, other) if other else piece)
        width = wanted

        def plan(spots_ref, sources, targets):
            return [
                (
                    source.at[0, :, at * width : (at + 1) * width],
                    targets[at].at[spots_ref[other]],
                )
                for other, source in enumerate(sources)
                for at in range(len(weights))
            ]

        spots = jnp.stack([corner ^ other for other in range(PLANE)])
        shape = (PLANE, rows // 2, width)
        return assemble(plan, PLANE * len(weights), spots, arrived, [shape] * len(weights))

    def gather_units(self, plane):
        core = lax.axis_index("tensor")
        _, rows, columns = plane.shape
        own = lax.all_gather(plane, "dp", axis=0, tiled=True, axis_index_groups=self.columns)

        def plan(spots_ref, sources, targets):
            return [(sources[at], targets[0].at[:, spots_ref[at]]) for at in range(2)]

        (whole,) = assemble(
            plan,
            2,
            jnp.stack([core, 1 - core]),
            [own, swap_cores(own)],
            [(self.devices, 2, rows, columns)],
        )
        return whole.reshape(-1, columns)

    def sum_units(self, part):
        core = lax.axis_index("tensor")
        rows, columns = part.shape[0] // self.devices // 2, part.shape[1]
        parts = part.reshape(self.devices, 2, rows, columns)
        keep = lax.dynamic_index_in_dim(parts, core, 1, False)
        give = low(lax.dynamic_index_in_dim(parts, 1 - core, 1, False))
        sums = low(wide(keep) + wide(swap_cores(give)))
        return lax.psum_scatter(
            sums, "dp", scatter_dimension=0, tiled=True, axis_index_groups=self.columns
        )

    def return_units(self, total):
        core = lax.axis_index("tensor")
        _, corner = self.place()
        _, rows, columns = total.shape
        quarters = jnp.zeros(total.shape, LOW)
        for other in range(PLANE):
            piece = lax.dynamic_slice_in_dim(total, corner ^ other, 1, 0)
            if other:
                piece = self.swap(piece, other)
            quarters = lax.dynamic_update_slice_in_dim(quarters, piece, corner ^ other, 0)
        keep = lax.dynamic_slice_in_dim(quarters, 2 * core, 2, 0)
        give = lax.dynamic_slice_in_dim(quarters, 2 - 2 * core, 2, 0)
        halves = order_cores(keep, swap_cores(give), axis=1)
        return wide(jnp.concatenate([halves[0], halves[1]], axis=1))

    def gather_gains(self, gains):
        level, corner = self.place()
        count, width = gains.shape
        pair = [gains, self.swap(gains, 1)]
        quad = jnp.stack(pair, axis=0)
        quad = jnp.concatenate([quad, self.swap(quad, 2)], axis=0)
        found = jnp.concatenate(self.ring_slots(quad), axis=0)
        found = found.reshape(self.devices, count * width)
        origin = jnp.arange(self.devices, dtype=jnp.int32)
        spot = ((level - origin // PLANE) % self.planes) * PLANE + ((origin % PLANE) ^ corner)
        choose = (spot[:, None] == origin[None, :]).astype(LOW)
        whole = jnp.dot(choose, found, preferred_element_type=jnp.float32)
        return jnp.swapaxes(whole.reshape(self.devices, count, width), 0, 1).reshape(count, -1)

    def sum_gains(self, part):
        total = part + swap_cores(part)
        total = total + self.swap(total, 1)
        total = total + self.swap(total, 2)
        slots = self.ring_slots(total)
        whole = slots[0]
        for slot in slots[1:]:
            whole = whole + slot
        width = whole.shape[1] // self.devices
        return lax.dynamic_slice(whole, (0, lax.axis_index("dp") * width), (part.shape[0], width))


def shards(
    links,
    tokens,
    cotangent,
    segments,
    query_weight,
    key_weight,
    value_weight,
    out_weight,
    gate_weight,
    up_weight,
    down_weight,
    norm_gains,
    query_moment,
    key_moment,
    value_moment,
    out_moment,
    gate_moment,
    up_moment,
    down_moment,
    gains_moment,
    query_square,
    key_square,
    value_square,
    out_square,
    gate_square,
    up_square,
    down_square,
    gains_square,
):
    lowtype = LOW
    core = lax.axis_index("tensor")
    rows = tokens.shape[0]
    seq_rows = 2 * rows

    def rows_of(values, which):
        return lax.dynamic_slice_in_dim(values, which * rows, rows, 0)

    def sum_plane_tokens(part):
        return links.plane_sum([part[rows * k : rows * (k + 1)] for k in range(PLANE)])

    gain_all = links.gather_gains(norm_gains.astype(lowtype))
    gain_one = gain_all[0]
    gain_two = gain_all[1]
    query_cols, key_cols = query_weight.shape[1], key_weight.shape[1]
    into_cols = query_cols + 2 * key_cols
    attn_weight = jnp.concatenate(
        [low(query_weight), low(key_weight), low(value_weight), low(out_weight)], axis=1
    )
    planes = links.spread_units([down_weight, gate_weight, up_weight])
    (into_all, out_all), gathered = links.gather_rows(attn_weight, into_cols, planes[0])
    down_all, gate_all, up_all = [links.gather_units(plane) for plane in planes]
    upstream = jnp.concatenate(links.plane_gather(after(cotangent, gathered)), axis=0)

    inputs = tokens.astype(jnp.float32)
    inverse_one = lax.rsqrt(jnp.mean(inputs * inputs, axis=1, keepdims=True) + NORM_EPS)
    normed_one = (inputs * inverse_one * gain_one).astype(lowtype)
    normed_one_all = order_cores(normed_one, swap_cores(normed_one))
    segment = segments[0]
    cosine, sine = rope_tables(segment)
    into = project(normed_one_all, into_all, cosine, sine, query_cols + key_cols)
    attended, log_totals = attend(into, segment, query_cols)
    attn_other = contract_cols(rows_of(attended, 1 - core), out_all).astype(lowtype)
    attn_own = contract_cols(rows_of(attended, core), out_all)
    hidden_state = inputs + (attn_own + swap_cores(attn_other).astype(jnp.float32))

    inverse_two = lax.rsqrt(jnp.mean(hidden_state * hidden_state, axis=1, keepdims=True) + NORM_EPS)
    normed_two = (hidden_state * inverse_two * gain_two).astype(lowtype)
    normed = jnp.concatenate(links.plane_gather(normed_two), axis=0)
    gate = jnp.dot(normed, gate_all, preferred_element_type=jnp.float32)
    upper = jnp.dot(normed, up_all, preferred_element_type=jnp.float32)
    grad_inner = jnp.dot(upstream, down_all, preferred_element_type=jnp.float32)
    sigma = jax.nn.sigmoid(gate)
    inner = low(gate * sigma * upper)
    grad_gate = low(grad_inner * upper * sigma * (1.0 + gate * (1.0 - sigma)))
    grad_upper = low(grad_inner * gate * sigma)
    grad_normed_two = sum_plane_tokens(
        contract_cols(grad_gate, gate_all) + contract_cols(grad_upper, up_all)
    )
    down_sum = links.sum_units(contract_rows(upstream, inner))
    gate_sum = links.sum_units(contract_rows(normed, grad_gate))
    up_sum = links.sum_units(contract_rows(normed, grad_upper))
    ffn_sum = sum_plane_tokens(after(contract_cols(inner, down_all), grad_normed_two))
    activations = (hidden_state + ffn_sum).astype(lowtype)
    down_shard = links.return_units(down_sum)
    gate_shard = links.return_units(gate_sum)
    up_shard = links.return_units(up_sum)

    hidden_back, gain_two_grad = norm_back(hidden_state, inverse_two, gain_two, grad_normed_two)
    hidden_grad = cotangent.astype(jnp.float32) + hidden_back
    attn_grad_low = hidden_grad.astype(lowtype)
    attn_grad_all = order_cores(attn_grad_low, swap_cores(attn_grad_low))
    attended_grad = jnp.dot(attn_grad_all, out_all, preferred_element_type=jnp.float32).astype(
        lowtype
    )
    out_grad_full = contract_rows(attn_grad_all, attended)
    out_shard = links.scatter_rows(after(out_grad_full, ffn_sum))
    into_back = jnp.concatenate(
        attend_back(into, attended_grad, log_totals, cosine, sine, segment), axis=1
    )
    into_shard = links.scatter_rows(contract_rows(normed_one_all, into_back))
    query_shard = into_shard[:, :query_cols]
    key_shard = into_shard[:, query_cols : query_cols + key_cols]
    value_shard = into_shard[:, query_cols + key_cols :]
    normed_other = contract_cols(rows_of(into_back, 1 - core), into_all).astype(lowtype)
    normed_own = contract_cols(rows_of(into_back, core), into_all)
    grad_normed_one = normed_own + swap_cores(normed_other).astype(jnp.float32)
    input_back, gain_one_grad = norm_back(inputs, inverse_one, gain_one, grad_normed_one)
    input_grad = hidden_grad + input_back
    gains_shard = links.sum_gains(jnp.stack([gain_one_grad, gain_two_grad], axis=0))
    q_all = adam(query_weight, query_shard, query_moment, query_square, RATE_MAIN, DECAY_RATE)
    k_all = adam(key_weight, key_shard, key_moment, key_square, RATE_MAIN, DECAY_RATE)
    v_all = adam(value_weight, value_shard, value_moment, value_square, RATE_MAIN, DECAY_RATE)
    o_all = adam(out_weight, out_shard, out_moment, out_square, RATE_OUT, DECAY_RATE)
    g_all = adam(gate_weight, gate_shard, gate_moment, gate_square, RATE_MAIN, DECAY_RATE)
    u_all = adam(up_weight, up_shard, up_moment, up_square, RATE_MAIN, DECAY_RATE)
    d_all = adam(down_weight, down_shard, down_moment, down_square, RATE_DOWN, DECAY_RATE)
    n_all = adam(norm_gains, gains_shard, gains_moment, gains_square, RATE_GAINS, 0.0)
    return (
        activations,
        input_grad,
        q_all[0],
        q_all[1],
        q_all[2],
        q_all[3],
        k_all[0],
        k_all[1],
        k_all[2],
        k_all[3],
        v_all[0],
        v_all[1],
        v_all[2],
        v_all[3],
        o_all[0],
        o_all[1],
        o_all[2],
        o_all[3],
        g_all[0],
        g_all[1],
        g_all[2],
        g_all[3],
        u_all[0],
        u_all[1],
        u_all[2],
        u_all[3],
        d_all[0],
        d_all[1],
        d_all[2],
        d_all[3],
        n_all[0],
        n_all[1],
        n_all[2],
        n_all[3],
    )


def solution(mesh):
    in_specs = (
        P(("dp", "tensor"), None),
        P(("dp", "tensor"), None),
        P("dp", None),
        P("dp", "tensor"),
        P("dp", "tensor"),
        P("dp", "tensor"),
        P("dp", "tensor"),
        P("dp", "tensor"),
        P("dp", "tensor"),
        P("dp", "tensor"),
        P(None, "dp"),
        P("dp", "tensor"),
        P("dp", "tensor"),
        P("dp", "tensor"),
        P("dp", "tensor"),
        P("dp", "tensor"),
        P("dp", "tensor"),
        P("dp", "tensor"),
        P(None, "dp"),
        P("dp", "tensor"),
        P("dp", "tensor"),
        P("dp", "tensor"),
        P("dp", "tensor"),
        P("dp", "tensor"),
        P("dp", "tensor"),
        P("dp", "tensor"),
        P(None, "dp"),
    )
    out_specs = (
        P(("dp", "tensor"), None),
        P(("dp", "tensor"), None),
        P("dp", "tensor"),
        P("dp", "tensor"),
        P("dp", "tensor"),
        P("dp", "tensor"),
        P("dp", "tensor"),
        P("dp", "tensor"),
        P("dp", "tensor"),
        P("dp", "tensor"),
        P("dp", "tensor"),
        P("dp", "tensor"),
        P("dp", "tensor"),
        P("dp", "tensor"),
        P("dp", "tensor"),
        P("dp", "tensor"),
        P("dp", "tensor"),
        P("dp", "tensor"),
        P("dp", "tensor"),
        P("dp", "tensor"),
        P("dp", "tensor"),
        P("dp", "tensor"),
        P("dp", "tensor"),
        P("dp", "tensor"),
        P("dp", "tensor"),
        P("dp", "tensor"),
        P("dp", "tensor"),
        P("dp", "tensor"),
        P("dp", "tensor"),
        P("dp", "tensor"),
        P(None, "dp"),
        P(None, "dp"),
        P(None, "dp"),
        P(None, "dp"),
    )
    links = Links(mesh.shape["dp"])
    return jax.shard_map(functools.partial(shards, links), mesh=mesh, in_specs=in_specs, out_specs=out_specs, check_vma=False)
```

```python
import functools
import math

import jax
import jax.numpy as jnp
from jax import lax
from jax.experimental import pallas as pl
from jax.experimental.pallas import tpu as pltpu
from jax.sharding import PartitionSpec as P

HEAD = 64
STEP = 10


NORM_EPS = 1e-05
NEG_LARGE = -1000000000.0
BETA_FIRST = 0.9
BETA_SECOND = 0.95
ADAM_EPS = 1e-08
DECAY_RATE = 0.1
RATE_MAIN = 0.02
RATE_OUT = 0.15
RATE_DOWN = 0.015
RATE_GAINS = 0.6


def rope_tables(segment):
    length = segment.shape[0]
    order = jnp.arange(length, dtype=jnp.int32)
    before = jnp.sum((segment[None, :] < segment[:, None]).astype(jnp.int32), axis=1)
    place = (order - before).astype(jnp.float32)
    half = HEAD // 2
    freq = jnp.exp(jnp.arange(half, dtype=jnp.float32) * (-2.0 * math.log(10000.0) / HEAD))
    angle = place[:, None] * freq[None, :]
    cosine, sine = jnp.cos(angle), jnp.sin(angle)
    return (
        jnp.concatenate([cosine] * 4, axis=1),
        jnp.concatenate([-sine, sine, -sine, sine], axis=1),
    )


def contract_rows(left, right):
    return lax.dot_general(
        left, right, (((0,), (0,)), ((), ())), preferred_element_type=jnp.float32
    )


def contract_cols(left, right):
    return lax.dot_general(
        left, right, (((1,), (1,)), ((), ())), preferred_element_type=jnp.float32
    )


def adam(weight, grad, moment, square, rate, decay):
    moment_new = BETA_FIRST * moment + (1.0 - BETA_FIRST) * grad
    square_new = BETA_SECOND * square + (1.0 - BETA_SECOND) * grad * grad
    direction = (
        moment_new
        / (1.0 - BETA_FIRST**STEP)
        / (jnp.sqrt(square_new / (1.0 - BETA_SECOND**STEP)) + ADAM_EPS)
    )
    return (grad, moment_new, square_new, weight - rate * (direction + decay * weight))


LOW = jnp.bfloat16
PLANE = 4
LANES = 128
TILE = 256
VMEM_LIMIT = 48 * 1024 * 1024
SMALL_COST = pl.CostEstimate(flops=1024, bytes_accessed=1024, transcendentals=0)
LARGE_COST = pl.CostEstimate(flops=1 << 35, bytes_accessed=1 << 20, transcendentals=0)


def swap_cores(block):
    return lax.ppermute(block, "tensor", [(0, 1), (1, 0)])


def late(kernel, count, *refs):
    ins, rest = refs[: count[0]], refs[count[0] + count[1] :]
    kernel(*ins, *rest)


def call(kernel, waits, operands, *, in_specs, cost=LARGE_COST, **options):
    place = pl.BlockSpec(memory_space=pltpu.HBM)
    return pl.pallas_call(
        functools.partial(late, kernel, (len(operands), len(waits))),
        in_specs=list(in_specs) + [place] * len(waits),
        compiler_params=pltpu.CompilerParams(vmem_limit_bytes=VMEM_LIMIT),
        cost_estimate=cost,
        **options,
    )(*operands, *waits)


def lane_of(shape):
    return lax.broadcasted_iota(jnp.int32, shape, len(shape) - 1)


def turn_heads(values, cosine, sine):
    first = lane_of(values.shape) % HEAD < HEAD // 2
    ahead = pltpu.roll(values, LANES - HEAD // 2, 1)
    behind = pltpu.roll(values, HEAD // 2, 1)
    return values * cosine + jnp.where(first, ahead, behind) * sine


def project_kernel(heads, normed_ref, weight_ref, cosine_ref, sine_ref, out_ref):
    part = jnp.dot(normed_ref[...], weight_ref[...], preferred_element_type=jnp.float32)
    cosine, sine = cosine_ref[...], sine_ref[...]
    step = pl.program_id(0)
    for at in range(0, part.shape[1], LANES):
        piece = part[:, at : at + LANES]
        turned = turn_heads(piece, cosine, sine)
        keep = step * part.shape[1] + at >= heads
        out_ref[:, at : at + LANES] = jnp.where(keep, piece, turned).astype(LOW)


def project(normed, weight, cosine, sine, turned, waits=()):
    rows, depth = normed.shape
    columns = weight.shape[1]
    block = 2 * LANES
    return call(
        functools.partial(project_kernel, turned),
        waits,
        (normed, weight, cosine, sine),
        cost=SMALL_COST,
        grid=(columns // block,),
        in_specs=[
            pl.BlockSpec((rows, depth), lambda i: (0, 0)),
            pl.BlockSpec((depth, block), lambda i: (0, i)),
            pl.BlockSpec((rows, LANES), lambda i: (0, 0)),
            pl.BlockSpec((rows, LANES), lambda i: (0, 0)),
        ],
        out_specs=pl.BlockSpec((rows, block), lambda i: (0, i)),
        out_shape=jax.ShapeDtypeStruct((rows, columns), LOW),
    )


def double(values, group):
    low_half = lane_of(values.shape) < HEAD
    other = pltpu.roll(values.astype(jnp.float32), HEAD, 1).astype(values.dtype)
    return jnp.where(low_half == (group == 0), values, other)


def set_bias(across_ref, down_ref, bias):
    rows = bias.shape[0]
    row = lax.broadcasted_iota(jnp.int32, (rows, rows), 0)
    column = lax.broadcasted_iota(jnp.int32, (rows, rows), 1)
    allowed = (down_ref[...] == across_ref[...]) & (column <= row)
    bias[...] = jnp.where(allowed, 0.0, NEG_LARGE)


def halves_of(block):
    low_half = lane_of(block.shape) < HEAD
    zero = jnp.zeros_like(block)
    return jnp.where(low_half, block, zero), jnp.where(low_half, zero, block)


def dot_last(left, right):
    return lax.dot_general(
        left, right, (((1,), (1,)), ((), ())), preferred_element_type=jnp.float32
    )


def dot_first(left, right):
    return lax.dot_general(
        left, right, (((0,), (0,)), ((), ())), preferred_element_type=jnp.float32
    )


def attend_kernel(
    group, query_ref, key_ref, value_ref, across_ref, down_ref, out_ref, total_ref, bias, keys, values
):
    step = pl.program_id(0)
    rows = query_ref.shape[0]

    @pl.when(step == 0)
    def _():
        set_bias(across_ref, down_ref, bias)
        total_ref[...] = jnp.zeros_like(total_ref)
        keys[...] = double(key_ref[...], group)
        values[...] = double(value_ref[...], group)

    for start in range(0, rows, TILE):
        stop = start + TILE
        query = query_ref[start:stop, :] * jnp.asarray(HEAD**-0.5, LOW)
        key, value = keys[:stop, :], values[:stop, :]
        shade = bias[start:stop, :stop]
        outs = []
        lane = lane_of((TILE, LANES))
        totals = total_ref[start:stop, :]
        for side, part in enumerate(halves_of(query)):
            score = dot_last(part, key) + shade
            largest = jnp.max(score, axis=1, keepdims=True)
            expo = jnp.exp(score - largest)
            total = jnp.sum(expo, axis=1, keepdims=True)
            probs = (expo * (1.0 / total)).astype(LOW)
            outs.append(jnp.dot(probs, value, preferred_element_type=jnp.float32))
            totals = jnp.where(lane == 2 * step + side, largest + jnp.log(total), totals)
        total_ref[start:stop, :] = totals
        out_ref[start:stop, :] = jnp.where(lane < HEAD, outs[0], outs[1]).astype(LOW)


def attend(into, segment, query_cols, group, waits=()):
    rows = into.shape[0]
    pairs = query_cols // LANES
    here = pairs // 2
    return call(
        functools.partial(attend_kernel, group),
        waits,
        (into, into, into, segment[None, :], segment[:, None]),
        cost=SMALL_COST,
        grid=(here,),
        in_specs=[
            pl.BlockSpec((rows, LANES), lambda i: (0, group * here + i)),
            pl.BlockSpec((rows, LANES), lambda i: (0, pairs)),
            pl.BlockSpec((rows, LANES), lambda i: (0, pairs + 1)),
            pl.BlockSpec((1, rows), lambda i: (0, 0)),
            pl.BlockSpec((rows, 1), lambda i: (0, 0)),
        ],
        out_specs=[
            pl.BlockSpec((rows, LANES), lambda i: (0, i)),
            pl.BlockSpec((rows, LANES), lambda i: (0, 0)),
        ],
        out_shape=[
            jax.ShapeDtypeStruct((rows, query_cols // 2), LOW),
            jax.ShapeDtypeStruct((rows, LANES), jnp.float32),
        ],
        scratch_shapes=[
            pltpu.VMEM((rows, rows), jnp.float32),
            pltpu.VMEM((rows, LANES), LOW),
            pltpu.VMEM((rows, LANES), LOW),
        ],
    )


def attend_back_kernel(
    group,
    query_ref,
    key_ref,
    value_ref,
    upstream_ref,
    total_ref,
    cosine_ref,
    sine_ref,
    across_ref,
    down_ref,
    before_ref,
    query_back_ref,
    rest_ref,
    bias,
    keys,
    values,
    key_sum,
    value_sum,
):
    step = pl.program_id(0)
    rows = query_ref.shape[0]

    @pl.when(step == 0)
    def _():
        set_bias(across_ref, down_ref, bias)
        keys[...] = double(key_ref[...], group)
        values[...] = double(value_ref[...], group)
        key_sum[...] = jnp.zeros_like(key_sum)
        value_sum[...] = jnp.zeros_like(value_sum)

    scale = jnp.asarray(HEAD**-0.5, LOW)
    for start in range(0, rows, TILE):
        stop = start + TILE
        query = query_ref[start:stop, :] * scale
        upstream = upstream_ref[start:stop, :]
        key, value = keys[:stop, :], values[:stop, :]
        shade = bias[start:stop, :stop]
        lane = lane_of((TILE, LANES))
        backs = []
        key_part = value_part = None
        for side, (part, grad) in enumerate(zip(halves_of(query), halves_of(upstream))):
            log_total = jnp.sum(
                jnp.where(lane == 2 * step + side, total_ref[start:stop, :], 0.0),
                axis=1,
                keepdims=True,
            )
            probs = jnp.exp(dot_last(part, key) + shade - log_total)
            value_here = dot_first(probs.astype(LOW), grad)
            probs_grad = dot_last(grad, value)
            delta = jnp.sum(probs * probs_grad, axis=1, keepdims=True)
            score_grad = (probs * (probs_grad - delta)).astype(LOW)
            backs.append(jnp.dot(score_grad, key, preferred_element_type=jnp.float32))
            key_here = dot_first(score_grad, part)
            key_part = key_here if key_part is None else key_part + key_here
            value_part = value_here if value_part is None else value_part + value_here
        key_sum[:stop, :] += key_part
        value_sum[:stop, :] += value_part
        back = jnp.where(lane < HEAD, backs[0], backs[1]) * HEAD**-0.5
        back = turn_heads(back, cosine_ref[start:stop, :], -sine_ref[start:stop, :])
        query_back_ref[start:stop, :] = back.astype(LOW)

    @pl.when(step == pl.num_programs(0) - 1)
    def _():
        key_back = key_sum[...] + pltpu.roll(key_sum[...], HEAD, 1)
        key_back = turn_heads(key_back, cosine_ref[...], -sine_ref[...]).astype(LOW)
        value_back = (value_sum[...] + pltpu.roll(value_sum[...], HEAD, 1)).astype(LOW)
        first = (lane_of(key_back.shape) < HEAD) & (group > 0)
        rest_ref[:, :LANES] = jnp.where(first, before_ref[:, :LANES], key_back)
        rest_ref[:, LANES:] = jnp.where(first, before_ref[:, LANES:], value_back)


def attend_back(into, upstream, log_totals, cosine, sine, segment, before, group, waits=()):
    rows, query_cols = upstream.shape
    pairs = query_cols // LANES
    here = pairs // 2
    whole = lambda width: pl.BlockSpec((rows, width), lambda i: (0, 0))
    return call(
        functools.partial(attend_back_kernel, group),
        waits,
        (into, into, into, upstream, log_totals, cosine, sine, segment[None, :], segment[:, None], before),
        grid=(here,),
        in_specs=[
            pl.BlockSpec((rows, LANES), lambda i: (0, group * here + i)),
            pl.BlockSpec((rows, LANES), lambda i: (0, pairs)),
            pl.BlockSpec((rows, LANES), lambda i: (0, pairs + 1)),
            pl.BlockSpec((rows, LANES), lambda i: (0, group * here + i)),
            whole(LANES),
            whole(LANES),
            whole(LANES),
            pl.BlockSpec((1, rows), lambda i: (0, 0)),
            whole(1),
            whole(2 * LANES),
        ],
        out_specs=[pl.BlockSpec((rows, LANES), lambda i: (0, i)), whole(2 * LANES)],
        out_shape=[
            jax.ShapeDtypeStruct((rows, query_cols // 2), LOW),
            jax.ShapeDtypeStruct((rows, 2 * LANES), LOW),
        ],
        scratch_shapes=[
            pltpu.VMEM((rows, rows), jnp.float32),
            pltpu.VMEM((rows, LANES), LOW),
            pltpu.VMEM((rows, LANES), LOW),
            pltpu.VMEM((rows, LANES), jnp.float32),
            pltpu.VMEM((rows, LANES), jnp.float32),
        ],
    )


def across_kernel(cuts, left_ref, right_ref, *out_refs):
    part = dot_last(left_ref[...], right_ref[...]).astype(LOW)
    start = 0
    for rows, out_ref in zip(cuts, out_refs):
        out_ref[...] = part[start : start + rows]
        start += rows


def across(left, right, first, cuts, waits=()):
    depth, columns = right.shape[1], right.shape[0]
    rows = sum(cuts)
    block = min(columns, 4 * LANES)
    assert first % rows == 0
    return call(
        functools.partial(across_kernel, cuts),
        waits,
        (left, right),
        grid=(columns // block,),
        in_specs=[
            pl.BlockSpec((rows, depth), lambda i: (first // rows, 0)),
            pl.BlockSpec((block, depth), lambda i: (i, 0)),
        ],
        out_specs=[pl.BlockSpec((cut, block), lambda i: (0, i)) for cut in cuts],
        out_shape=[jax.ShapeDtypeStruct((cut, columns), LOW) for cut in cuts],
    )


def plain_kernel(left_ref, right_ref, out_ref):
    out_ref[...] = jnp.dot(
        left_ref[...], right_ref[...], preferred_element_type=jnp.float32
    ).astype(LOW)


def plain(left, right, waits=()):
    rows, depth = left.shape
    columns = right.shape[1]
    block = 2 * LANES
    return call(
        plain_kernel,
        waits,
        (left, right),
        grid=(columns // block,),
        in_specs=[
            pl.BlockSpec((rows, depth), lambda i: (0, 0)),
            pl.BlockSpec((depth, block), lambda i: (0, i)),
        ],
        out_specs=pl.BlockSpec((rows, block), lambda i: (0, i)),
        out_shape=jax.ShapeDtypeStruct((rows, columns), LOW),
    )


def join_kernel(first_ref, second_ref, far_one_ref, far_two_ref, one_ref, two_ref):
    half = far_one_ref.shape[0]
    one_ref[:half] = first_ref[:half]
    one_ref[half:] = low(wide(first_ref[half:]) + wide(far_two_ref[...]))
    two_ref[:half] = low(wide(second_ref[:half]) + wide(far_one_ref[...]))
    two_ref[half:] = second_ref[half:]


def join_sends(first, second, far_one, far_two, waits=()):
    rows, columns = first.shape
    block = min(columns, 4 * LANES) if columns % (4 * LANES) == 0 else 2 * LANES
    full = pl.BlockSpec((rows, block), lambda i: (0, i))
    part = pl.BlockSpec((rows // 2, block), lambda i: (0, i))
    shape = jax.ShapeDtypeStruct((rows, columns), LOW)
    return call(
        join_kernel,
        waits,
        (first, second, far_one, far_two),
        cost=SMALL_COST,
        grid=(columns // block,),
        in_specs=[full, full, part, part],
        out_specs=[full, full],
        out_shape=[shape, shape],
    )


def norm_back_kernel(count, *refs):
    grads = refs[:count]
    values_ref, gain_ref, plus_ref, sum_ref, low_ref, gain_grad_ref = refs[count:]
    grad = sum(wide(ref[...]) for ref in grads)
    values = wide(values_ref[...])
    mean = jnp.mean(values * values, axis=1, keepdims=True)
    inverse = lax.rsqrt(mean + NORM_EPS)
    weighted = gain_ref[...] * grad
    across_mean = jnp.mean(weighted * values, axis=1, keepdims=True)
    back = inverse * weighted - values * (inverse * inverse * inverse) * across_mean
    total = wide(plus_ref[...]) + back
    sum_ref[...] = total
    low_ref[...] = low(total)

    @pl.when(pl.program_id(0) == 0)
    def _():
        gain_grad_ref[...] = jnp.zeros_like(gain_grad_ref)

    gain_grad_ref[...] += jnp.sum(grad * values * inverse, axis=0, keepdims=True)


def norm_back(grads, values, gain, plus, waits=()):
    rows, columns = values.shape
    block = LANES
    row = by_rows(block, columns)
    line = pl.BlockSpec((1, columns), lambda i: (0, 0))
    return call(
        functools.partial(norm_back_kernel, len(grads)),
        waits,
        (*grads, values, gain[None, :], plus),
        cost=SMALL_COST,
        grid=(rows // block,),
        in_specs=[row] * len(grads) + [row, line, row],
        out_specs=[row, row, line],
        out_shape=[
            jax.ShapeDtypeStruct((rows, columns), jnp.float32),
            jax.ShapeDtypeStruct((rows, columns), LOW),
            jax.ShapeDtypeStruct((1, columns), jnp.float32),
        ],
    )


def gate_up_kernel(normed_ref, weight_ref, out_ref):
    out_ref[...] = jnp.dot(normed_ref[...], weight_ref[...], preferred_element_type=jnp.float32)


def hidden_kernel(upstream_ref, down_ref, gate_up_ref, inner_ref, grads_ref):
    width = down_ref.shape[1]
    grad = jnp.dot(upstream_ref[...], down_ref[...], preferred_element_type=jnp.float32)
    gate = gate_up_ref[:, :width]
    upper = gate_up_ref[:, width:]
    sigma = 1.0 / (1.0 + jnp.exp(-gate))
    active = gate * sigma
    inner_ref[...] = (active * upper).astype(LOW)
    slope = sigma * (1.0 + gate * (1.0 - sigma))
    grads_ref[:, :width] = (grad * upper * slope).astype(LOW)
    grads_ref[:, width:] = (grad * active).astype(LOW)


def held(array):
    return pl.BlockSpec(array.shape, lambda i: (0, 0), pipeline_mode=pl.Buffered(1))


def by_rows(block, width):
    return pl.BlockSpec((block, width), lambda i: (i, 0))


def gate_and_up(normed, weight, waits=()):
    rows, depth = normed.shape
    columns = weight.shape[1]
    return call(
        gate_up_kernel,
        waits,
        (normed, weight),
        grid=(rows // TILE,),
        in_specs=[by_rows(TILE, depth), held(weight)],
        out_specs=by_rows(TILE, columns),
        out_shape=jax.ShapeDtypeStruct((rows, columns), jnp.float32),
    )


def hidden(upstream, down, gate_up, waits=()):
    rows, depth = upstream.shape
    width = down.shape[1]
    return call(
        hidden_kernel,
        waits,
        (upstream, down, gate_up),
        grid=(rows // TILE,),
        in_specs=[by_rows(TILE, depth), held(down), by_rows(TILE, 2 * width)],
        out_specs=[by_rows(TILE, width), by_rows(TILE, 2 * width)],
        out_shape=[
            jax.ShapeDtypeStruct((rows, width), LOW),
            jax.ShapeDtypeStruct((rows, 2 * width), LOW),
        ],
    )


def inner_kernel(left_ref, right_ref, out_ref):
    out_ref[...] = dot_first(left_ref[...], right_ref[...]).astype(LOW)


def inner_rows(left, right, waits=()):
    depth, rows = left.shape
    columns = right.shape[1]
    block = 2 * LANES
    return call(
        inner_kernel,
        waits,
        (left, right),
        grid=(rows // block,),
        in_specs=[pl.BlockSpec((depth, block), lambda i: (0, i)), held(right)],
        out_specs=pl.BlockSpec((block, columns), lambda i: (i, 0)),
        out_shape=jax.ShapeDtypeStruct((rows, columns), LOW),
    )


def put_halves(core_ref, part, keep_ref, give_ref):
    rows = keep_ref.shape[1]
    first = core_ref[0] == 0
    for at in range(keep_ref.shape[0]):
        start = 2 * rows * at
        top, bottom = part[start : start + rows], part[start + rows : start + 2 * rows]
        keep_ref[at] = jnp.where(first, top, bottom)
        give_ref[at] = jnp.where(first, bottom, top)


def unit_grads_kernel(
    blocks,
    core_ref,
    upstream_ref,
    inner_ref,
    normed_ref,
    grads_ref,
    down_keep_ref,
    down_give_ref,
    keep_ref,
    give_ref,
):
    step = pl.program_id(0)

    @pl.when(step < blocks)
    def _():
        part = dot_first(upstream_ref[...], inner_ref[...]).astype(LOW)
        put_halves(core_ref, part, down_keep_ref, down_give_ref)

    @pl.when(step >= blocks)
    def _():
        part = dot_first(normed_ref[...], grads_ref[...]).astype(LOW)
        put_halves(core_ref, part, keep_ref, give_ref)


def unit_grads(upstream, inner, normed, grads, rows, waits=()):
    depth, total = upstream.shape
    block = 2 * LANES
    blocks, lots = total // block, block // rows // 2
    core = lax.axis_index("tensor").astype(jnp.int32).reshape(1)
    early = lambda i: jnp.minimum(i, blocks - 1)
    late_on = lambda i: jnp.maximum(i - blocks, 0)
    out = lambda width, when: pl.BlockSpec((lots, rows, width), lambda i: (when(i), 0, 0))
    shape = lambda width: jax.ShapeDtypeStruct((total // rows // 2, rows, width), LOW)
    widths = inner.shape[1], grads.shape[1]
    return call(
        functools.partial(unit_grads_kernel, blocks),
        waits,
        (core, upstream, inner, normed, grads),
        grid=(2 * blocks,),
        in_specs=[
            pl.BlockSpec(memory_space=pltpu.SMEM),
            pl.BlockSpec((depth, block), lambda i: (0, early(i))),
            held(inner),
            pl.BlockSpec((depth, block), lambda i: (0, late_on(i))),
            held(grads),
        ],
        out_specs=[out(widths[0], early)] * 2 + [out(widths[1], late_on)] * 2,
        out_shape=[shape(widths[0])] * 2 + [shape(widths[1])] * 2,
    )


def hold_kernel(*refs):
    half = len(refs) // 2
    for source, target in zip(refs[:half], refs[half:]):
        target[...] = source[...]


def hold(values, waits=()):
    specs = [pl.BlockSpec(value.shape, lambda *_, rank=value.ndim: (0,) * rank) for value in values]
    return list(
        call(
            hold_kernel,
            waits,
            values,
            cost=SMALL_COST,
            grid=(1,),
            in_specs=specs,
            out_specs=specs,
            out_shape=[jax.ShapeDtypeStruct(value.shape, value.dtype) for value in values],
        )
    )


def nothing_kernel(*refs):
    del refs


def fence(values, waits=()):
    place = pl.BlockSpec(memory_space=pltpu.HBM)
    return list(
        pl.pallas_call(
            nothing_kernel,
            in_specs=[place] * (len(values) + len(waits)),
            out_specs=[place] * len(values),
            out_shape=[jax.ShapeDtypeStruct(value.shape, value.dtype) for value in values],
            input_output_aliases={at: at for at in range(len(values))},
            compiler_params=pltpu.CompilerParams(vmem_limit_bytes=1024 * 1024),
            cost_estimate=SMALL_COST,
        )(*values, *waits)
    )


def move_kernel(counts, cuts, extra, spots_ref, *refs):
    *blocks, sems = refs
    sources, targets = blocks[: len(counts)], blocks[len(counts) + extra :]
    copies, step = [], 0
    for count, source in zip(counts, sources):
        for at in range(count):
            for (left, right), target in zip(cuts, targets):
                part = source.at[at] if len(cuts) == 1 else source.at[at, :, left:right]
                copies.append(
                    pltpu.make_async_copy(part, target.at[spots_ref[step]], sems.at[len(copies)])
                )
            step += 1
    for copy in copies:
        copy.start()
    for copy in copies:
        copy.wait()


def move(blocks, spots, cuts=None, waits=()):
    counts = [block.shape[0] for block in blocks]
    rows, columns = blocks[0].shape[1:]
    ends = [0, *(cuts or []), columns]
    lots = list(zip(ends[:-1], ends[1:]))
    place = pl.BlockSpec(memory_space=pltpu.HBM)
    return pl.pallas_call(
        functools.partial(move_kernel, counts, lots, len(waits)),
        in_specs=[pl.BlockSpec(memory_space=pltpu.SMEM)] + [place] * (len(blocks) + len(waits)),
        out_specs=[place] * len(lots),
        out_shape=[
            jax.ShapeDtypeStruct((sum(counts), rows, right - left), LOW) for left, right in lots
        ],
        scratch_shapes=[pltpu.SemaphoreType.DMA((sum(counts) * len(lots),))],
        compiler_params=pltpu.CompilerParams(vmem_limit_bytes=1024 * 1024),
        cost_estimate=SMALL_COST,
    )(spots, *blocks, *waits)


def split_kernel(left_columns, whole_ref, left_ref, right_ref):
    left_ref[...] = whole_ref[:, :, :left_columns]
    right_ref[...] = whole_ref[:, :, left_columns:]


def split_columns(whole, left, waits=()):
    lots, rows, columns = whole.shape
    block = max(1, lots // 4)
    spec = lambda width: pl.BlockSpec((block, rows, width), lambda i: (i, 0, 0))
    shape = lambda width: jax.ShapeDtypeStruct((lots, rows, width), LOW)
    return call(
        functools.partial(split_kernel, left),
        waits,
        (whole,),
        cost=SMALL_COST,
        grid=(lots // block,),
        in_specs=[spec(columns)],
        out_specs=[spec(left), spec(columns - left)],
        out_shape=[shape(left), shape(columns - left)],
    )


def spread_kernel(cuts, extra, spots_ref, own_ref, other_ref, *refs):
    *targets, sems = refs[extra:]
    copies = []
    for at, source in enumerate((own_ref, other_ref)):
        for (left, right), target in zip(cuts, targets):
            copies.append(
                pltpu.make_async_copy(
                    source.at[:, :, left:right], target.at[:, spots_ref[at]], sems.at[len(copies)]
                )
            )
    for copy in copies:
        copy.start()
    for copy in copies:
        copy.wait()


def spread_halves(own, other, spots, cuts):
    count, rows, columns = own.shape
    ends = [0, *cuts, columns]
    lots = list(zip(ends[:-1], ends[1:]))
    place = pl.BlockSpec(memory_space=pltpu.HBM)
    return pl.pallas_call(
        functools.partial(spread_kernel, lots, 0),
        in_specs=[pl.BlockSpec(memory_space=pltpu.SMEM), place, place],
        out_specs=[place] * len(lots),
        out_shape=[
            jax.ShapeDtypeStruct((count, 2, rows, right - left), LOW) for left, right in lots
        ],
        scratch_shapes=[pltpu.SemaphoreType.DMA((2 * len(lots),))],
        compiler_params=pltpu.CompilerParams(vmem_limit_bytes=1024 * 1024),
        cost_estimate=SMALL_COST,
    )(spots, own, other)


def pick_kernel(count, spots_ref, *refs):
    del spots_ref
    for source, target in zip(refs[:count], refs[len(refs) - count :]):
        target[...] = source[0]


def pick(parts, spots, waits=()):
    lots, _, rows, columns = parts.shape
    count = spots.shape[0]
    place = pl.BlockSpec(memory_space=pltpu.HBM)
    return pl.pallas_call(
        functools.partial(pick_kernel, count),
        grid_spec=pltpu.PrefetchScalarGridSpec(
            num_scalar_prefetch=1,
            grid=(lots,),
            in_specs=[
                pl.BlockSpec(
                    (1, 1, rows, columns), lambda i, spots_ref, at=at: (i, spots_ref[at], 0, 0)
                )
                for at in range(count)
            ]
            + [place] * len(waits),
            out_specs=[
                pl.BlockSpec((1, rows, columns), lambda i, spots_ref: (i, 0, 0))
                for at in range(count)
            ],
        ),
        out_shape=[jax.ShapeDtypeStruct((lots, rows, columns), LOW)] * count,
        compiler_params=pltpu.CompilerParams(vmem_limit_bytes=VMEM_LIMIT),
        cost_estimate=SMALL_COST,
    )(spots, *[parts] * count, *waits)


def add_kernel(*refs):
    out_ref = refs[-1]
    start = 0
    for one_ref, two_ref in zip(refs[:-1:2], refs[1:-1:2]):
        stop = start + one_ref.shape[2]
        out_ref[:, :, start:stop] = low(wide(one_ref[...]) + wide(two_ref[...]))
        start = stop


def add_low(pairs, waits=()):
    lots, rows, _ = pairs[0][0].shape
    block = max(1, lots // 4)
    spec = lambda width: pl.BlockSpec((block, rows, width), lambda i: (i, 0, 0))
    arrays = [array for pair in pairs for array in pair]
    total = sum(one.shape[2] for one, _ in pairs)
    return call(
        add_kernel,
        waits,
        arrays,
        cost=SMALL_COST,
        grid=(lots // block,),
        in_specs=[spec(array.shape[2]) for array in arrays],
        out_specs=spec(total),
        out_shape=jax.ShapeDtypeStruct((lots, rows, total), LOW),
    )


def norm_kernel(values_ref, gain_ref, out_ref):
    values = wide(values_ref[...])
    mean = jnp.mean(values * values, axis=1, keepdims=True)
    out_ref[...] = low(values * lax.rsqrt(mean + NORM_EPS) * gain_ref[...])


def norm(values, gain, waits=()):
    rows, columns = values.shape
    row = by_rows(LANES, columns)
    return call(
        norm_kernel,
        waits,
        (values, gain[None, :]),
        cost=SMALL_COST,
        grid=(rows // LANES,),
        in_specs=[row, pl.BlockSpec((1, columns), lambda i: (0, 0))],
        out_specs=row,
        out_shape=jax.ShapeDtypeStruct((rows, columns), LOW),
    )


def order_rows(own, other):
    core = lax.axis_index("tensor").astype(jnp.int32)
    (whole,) = move([own[None], other[None]], jnp.stack([core, 1 - core]))
    return whole.reshape(-1, own.shape[1])


def pick_halves_kernel(count, half, spots_ref, *refs):
    del spots_ref
    targets = refs[count:]
    step = pl.program_id(0)
    targets[0][...] = refs[0][0]

    @pl.when(step < half)
    def _():
        for at in range(1, count):
            targets[2 * at - 1][...] = refs[at][0]

    @pl.when(step >= half)
    def _():
        for at in range(1, count):
            targets[2 * at][...] = refs[at][0]


def pick_halves(parts, spots):
    lots, _, rows, columns = parts.shape
    count, half = spots.shape[0], lots // 2
    spec = lambda where: pl.BlockSpec((1, rows, columns), where)
    shape = lambda size: jax.ShapeDtypeStruct((size, rows, columns), LOW)
    early = spec(lambda i, spots_ref: (jnp.minimum(i, half - 1), 0, 0))
    late_on = spec(lambda i, spots_ref: (jnp.maximum(i - half, 0), 0, 0))
    found = pl.pallas_call(
        functools.partial(pick_halves_kernel, count, half),
        grid_spec=pltpu.PrefetchScalarGridSpec(
            num_scalar_prefetch=1,
            grid=(lots,),
            in_specs=[
                pl.BlockSpec(
                    (1, 1, rows, columns), lambda i, spots_ref, at=at: (i, spots_ref[at], 0, 0)
                )
                for at in range(count)
            ],
            out_specs=[spec(lambda i, spots_ref: (i, 0, 0))] + [early, late_on] * (count - 1),
        ),
        out_shape=[shape(lots)] + [shape(half), shape(lots - half)] * (count - 1),
        compiler_params=pltpu.CompilerParams(vmem_limit_bytes=VMEM_LIMIT),
        cost_estimate=SMALL_COST,
    )(spots, *[parts] * count)
    return [block.reshape(-1, columns) for block in found]


def add_pairs_kernel(*refs):
    third = len(refs) // 3
    for one_ref, two_ref, out_ref in zip(refs[:third], refs[third : 2 * third], refs[2 * third :]):
        out_ref[...] = low(wide(one_ref[...]) + wide(two_ref[...]))


def add_pairs(ones, twos, waits=()):
    rows, columns = ones[0].shape
    block = columns // 2
    spec = pl.BlockSpec((rows, block), lambda i: (0, i))
    return call(
        add_pairs_kernel,
        waits,
        (*ones, *twos),
        cost=SMALL_COST,
        grid=(2,),
        in_specs=[spec] * (2 * len(ones)),
        out_specs=[spec] * len(ones),
        out_shape=[jax.ShapeDtypeStruct((rows, columns), LOW)] * len(ones),
    )


def part_rows(whole, waits=()):
    core = lax.axis_index("tensor").astype(jnp.int32)
    rows, columns = whole.shape[0] // 2, whole.shape[1]
    own, other = pick(whole.reshape(1, 2, rows, columns), jnp.stack([core, 1 - core]), waits)
    return own[0], other[0]


def wide(block):
    return block.astype(jnp.float32)


def low(block):
    return block.astype(LOW)


def order_cores(own, other, axis=0):
    return jnp.where(
        lax.axis_index("tensor") == 0,
        jnp.concatenate([own, other], axis=axis),
        jnp.concatenate([other, own], axis=axis),
    )


class Links:
    def __init__(self, devices):
        self.devices = devices
        self.planes = devices // PLANE
        self.pairs = {
            step: [(index, index ^ step) for index in range(devices)] for step in (1, 2, 3)
        }
        self.columns = [list(range(corner, devices, PLANE)) for corner in range(PLANE)]
        self.ring = [(index, (index + PLANE) % devices) for index in range(devices)]

    def swap(self, block, step):
        return lax.ppermute(block, "dp", self.pairs[step])

    def turn(self, block):
        return lax.ppermute(block, "dp", self.ring)

    def place(self):
        index = lax.axis_index("dp").astype(jnp.int32)
        return index // PLANE, index % PLANE

    def corner_spots(self):
        _, corner = self.place()
        return jnp.stack([corner ^ other for other in range(PLANE)])

    def shift(self, block, step):
        pairs = [(at, (at + PLANE * step) % self.devices) for at in range(self.devices)]
        return lax.ppermute(block, "dp", pairs)

    def gather_near(self, block):
        return [self.swap(block, 1), self.swap(block, 2)]

    def gather_far(self, first, second):
        half = first.shape[0] // 2
        return [self.swap(second[:half], 1), self.swap(first[half:], 2)]

    def sum_far(self, far_top, far_bottom):
        return [self.swap(far_top, 1), self.swap(far_bottom, 2)]

    def ring_start(self, sums, rows):
        level, _ = self.place()
        return lax.dynamic_slice_in_dim(sums, (level - 1) % self.planes * rows, rows, 0)

    def ring_step(self, total, sums, rows, step):
        level, _ = self.place()
        spot = (level - 1 - step) % self.planes * rows
        return wide(self.turn(low(total))) + lax.dynamic_slice_in_dim(sums, spot, rows, 0)

    def corners(self, part):
        rows, columns = part.shape[0] // self.devices, part.shape[1]
        parts = part.reshape(self.planes, PLANE, rows, columns)
        return pick_halves(parts, self.corner_spots())

    def sum_top(self, one_top, two_low):
        return [self.swap(one_top, 1), self.swap(two_low, 2)]

    def sum_low(self, one_low, two_top, far_one, far_two, waits=()):
        one, two = add_pairs([one_low, two_top], [far_two, far_one], waits)
        return [self.swap(one, 1), self.swap(two, 2)]

    def place_rows(self, rows, columns, bundles):
        level, corner = self.place()
        blocks, spots = [], []
        for start, parts in bundles:
            for other, lists in enumerate(parts):
                step = start
                for block in lists:
                    here = block.shape[0] // rows
                    for _ in range(here):
                        spots.append(((level - step) % self.planes) * PLANE + (corner ^ other))
                        step += 1
                    blocks.append(block.reshape(here, rows, columns))
        (whole,) = move(blocks, jnp.stack(spots))
        return whole.reshape(-1, columns)

    def cut_units(self, weights):
        core = lax.axis_index("tensor")
        rows, columns = weights[0].shape
        wanted = columns // 2
        pieces = jnp.stack(
            [
                jnp.concatenate(
                    [low(weight[:, half * wanted : (half + 1) * wanted]) for weight in weights],
                    axis=1,
                )
                for half in range(2)
            ],
            axis=0,
        ).reshape(2, 2, rows // 2, wanted * len(weights))
        keep = lax.dynamic_index_in_dim(pieces, core, 1, False)
        give = lax.dynamic_index_in_dim(pieces, 1 - core, 1, False)
        return keep, give

    def spread_units(self, keep, given):
        _, corner = self.place()
        quarters = order_cores(keep, given)
        arrived = []
        for other in range(PLANE):
            piece = lax.dynamic_slice_in_dim(quarters, corner ^ other, 1, 0)
            arrived.append(self.swap(piece, other) if other else piece)
        return arrived

    def place_plane(self, arrived, waits=()):
        return move(arrived, self.corner_spots(), None, waits)

    def gather_planes(self, plane):
        return lax.all_gather(plane, "dp", axis=0, tiled=True, axis_index_groups=self.columns)

    def place_units(self, own, other, cuts):
        core = lax.axis_index("tensor").astype(jnp.int32)
        parts = spread_halves(own, other, jnp.stack([core, 1 - core]), cuts)
        return [part.reshape(-1, part.shape[3]) for part in parts]

    def sum_planes(self, sums):
        return lax.psum_scatter(
            sums, "dp", scatter_dimension=0, tiled=True, axis_index_groups=self.columns
        )

    def return_units(self, total, waits=()):
        pieces = pick(total[None], self.corner_spots(), waits)
        arrived = [pieces[0]] + [self.swap(pieces[other], other) for other in (1, 2, 3)]
        return self.place_plane(arrived)[0]

    def join_units(self, quarters, count):
        core = lax.axis_index("tensor")
        keep = lax.dynamic_slice_in_dim(quarters, 2 * core, 2, 0)
        give = lax.dynamic_slice_in_dim(quarters, 2 - 2 * core, 2, 0)
        halves = order_cores(keep, swap_cores(give), axis=1)
        width = quarters.shape[2] // count
        return [
            wide(
                jnp.concatenate(
                    [halves[half][:, at * width : (at + 1) * width] for half in range(2)], axis=1
                )
            )
            for at in range(count)
        ]

    def gather_gains(self, corners, shape):
        level, corner = self.place()
        count, width = shape
        found = jnp.stack(corners, axis=0).reshape(self.devices, count * width)
        origin = jnp.arange(self.devices, dtype=jnp.int32)
        spot = ((origin % PLANE) ^ corner) * self.planes + (level - origin // PLANE) % self.planes
        choose = (spot[:, None] == origin[None, :]).astype(LOW)
        whole = jnp.dot(choose, found, preferred_element_type=jnp.float32)
        return jnp.swapaxes(whole.reshape(self.devices, count, width), 0, 1).reshape(count, -1)

    def own_gains(self, whole):
        width = whole.shape[1] // self.devices
        return lax.dynamic_slice(whole, (0, lax.axis_index("dp") * width), (whole.shape[0], width))


def shards(
    links,
    tokens,
    cotangent,
    segments,
    query_weight,
    key_weight,
    value_weight,
    out_weight,
    gate_weight,
    up_weight,
    down_weight,
    norm_gains,
    query_moment,
    key_moment,
    value_moment,
    out_moment,
    gate_moment,
    up_moment,
    down_moment,
    gains_moment,
    query_square,
    key_square,
    value_square,
    out_square,
    gate_square,
    up_square,
    down_square,
    gains_square,
):
    core = lax.axis_index("tensor")
    rows = tokens.shape[0]
    weight_rows, query_cols = query_weight.shape
    key_cols = key_weight.shape[1]
    into_cols = query_cols + 2 * key_cols
    units = gate_weight.shape[1]
    steps = links.planes

    def rows_of(values, which):
        return lax.dynamic_slice_in_dim(values, which * rows, rows, 0)

    def place_tokens(own, first, second, far_one, far_two):
        half, columns = rows // 2, own.shape[1]
        blocks = [block.reshape(-1, half, columns) for block in (own, first, second, far_one, far_two)]
        (whole,) = move(blocks, jnp.arange(2 * PLANE, dtype=jnp.int32))
        return whole.reshape(-1, columns)

    gains_low = low(norm_gains)
    into_weight = jnp.concatenate([low(query_weight), low(key_weight), low(value_weight)], axis=1)
    units_keep, units_give = links.cut_units([down_weight, gate_weight, up_weight])
    gain_slots = [gains_low] + [links.shift(gains_low, step) for step in range(1, steps)]
    slots = [into_weight, links.turn(into_weight)]
    units_given = swap_cores(units_give)
    gains_level = jnp.stack(gain_slots, axis=0)
    gains_level, units_given, slots[1] = fence([gains_level, units_given, slots[1]])

    gain_corners = [gains_level] + [links.swap(gains_level, other) for other in (1, 2, 3)]
    spread = links.spread_units(units_keep, units_given)
    for _ in range(2, steps):
        slots.append(links.turn(slots[-1]))
    values = fence([*spread[1:], slots[-1]])
    spread[1:], slots[-1] = values[:3], values[3]

    (units_plane,) = links.place_plane(spread)
    units_own = links.gather_planes(units_plane)
    out_slots = [low(out_weight)]
    for _ in range(1, steps):
        out_slots.append(links.turn(out_slots[-1]))

    group = max(1, steps // 2)
    into_one = jnp.concatenate(slots[:group], axis=0)
    into_two = jnp.concatenate(slots[group:], axis=0)
    near_one = links.gather_near(into_one)
    gain_all = links.gather_gains(gain_corners, norm_gains.shape)
    gain_one = gain_all[0]
    gain_two = gain_all[1]
    normed_one = norm(tokens, gain_one)
    normed_one_all = order_rows(normed_one, swap_cores(normed_one))
    segment = segments[0]
    cosine, sine = rope_tables(segment)
    near_one = fence(near_one, [normed_one_all, cosine, sine])
    far_one = links.gather_far(*near_one)
    near_two = links.gather_near(into_two)
    *far_one, near_a, near_b = fence([*far_one, *near_two])
    near_two = [near_a, near_b]
    far_two = fence(links.gather_far(*near_two))
    into_all = links.place_rows(
        weight_rows,
        into_cols,
        [
            (0, [[into_one], [near_one[0]], [near_one[1]], far_one]),
            (group, [[into_two], [near_two[0]], [near_two[1]], far_two]),
        ],
    )

    (out_bundle,) = fence([jnp.concatenate(out_slots, axis=0)], far_two)
    out_near = links.gather_near(out_bundle)
    into = project(normed_one_all, into_all, cosine, sine, query_cols + key_cols)
    attended_one, totals_one = attend(into, segment, query_cols, 0)
    out_near = fence(out_near, [attended_one])
    out_far = links.gather_far(*out_near)
    attended_two, totals_two = attend(into, segment, query_cols, 1, out_near)
    *out_far, cotangent_late = fence([*out_far, *hold([cotangent])], [attended_two])
    upstream_near = links.gather_near(cotangent_late)
    out_all = links.place_rows(
        weight_rows, query_cols, [(0, [[out_bundle], [out_near[0]], [out_near[1]], out_far])]
    )
    attended = jnp.concatenate([attended_one, attended_two], axis=1)
    attn_other = low(contract_cols(rows_of(attended, 1 - core), out_all))
    attn_own = contract_cols(rows_of(attended, core), out_all)
    hidden_state = wide(tokens) + (attn_own + wide(swap_cores(attn_other)))
    normed_two = norm(hidden_state, gain_two)

    normed_near = links.gather_near(normed_two)
    upstream_near = fence(upstream_near, [normed_two])
    (units_own,) = fence([units_own], upstream_near)
    units_other = swap_cores(units_own)
    *normed_near, units_other = fence([*normed_near, units_other])
    normed_far = links.gather_far(*normed_near)
    down_all, gate_up_all = links.place_units(units_own, units_other, [units // 2])
    normed_far = fence(normed_far, [down_all, gate_up_all])
    normed = place_tokens(normed_two, *normed_near, *normed_far)

    upstream_near = fence(upstream_near, normed_far)
    upstream_far = links.gather_far(*upstream_near)
    gate_up = gate_and_up(normed, gate_up_all)
    upstream = place_tokens(cotangent_late, *upstream_near, *upstream_far)
    inner, grads = hidden(upstream, down_all, gate_up)
    half = rows // 2
    back_far = across(grads, gate_up_all, 3 * rows, (half, half))
    back_far_sent = links.sum_far(*back_far)
    back_own, back_one, back_two = across(
        grads, gate_up_all, 0, (rows, rows, rows), [back_far[0]]
    )
    one_send, two_send = join_sends(back_one, back_two, *back_far_sent, [back_own])
    back_sent = [links.swap(one_send, 1), links.swap(two_send, 2)]
    down_keep, down_give, gate_up_keep, gate_up_give = unit_grads(
        upstream, inner, normed, grads, weight_rows // 2, [one_send, two_send]
    )
    hidden_grad, attn_grad_low, gain_two_grad = norm_back(
        [back_own, *back_sent], hidden_state, gain_two, cotangent, [down_keep]
    )
    attn_grad_other = swap_cores(attn_grad_low)
    down_other = swap_cores(down_give)
    gate_up_other = swap_cores(gate_up_give)
    ffn_own, one_top, one_low, two_top, two_low, *ffn_far = across(
        inner, down_all, 0, (rows, *[half] * 6), [attn_grad_low]
    )
    ffn_far_sent = links.sum_far(*ffn_far)
    ffn_near = [links.swap(one_top, 1), links.swap(two_low, 2)]
    unit_sums = add_low([(down_keep, down_other), (gate_up_keep, gate_up_other)], [ffn_own])
    units_sum = links.sum_planes(unit_sums)

    attn_grad_all = order_rows(attn_grad_low, attn_grad_other)
    attended_grad = plain(attn_grad_all, out_all, [ffn_own])
    out_own, one_top, one_low_out, two_top_out, two_low_out, *out_far = links.corners(
        inner_rows(attn_grad_all, attended, [attended_grad, unit_sums])
    )
    out_far_sent = links.sum_far(*out_far)
    out_top = links.sum_top(one_top, two_low_out)
    nothing = jnp.zeros((2 * rows, 2 * LANES), LOW)
    query_back_one, rest_back = attend_back(
        into,
        attended_grad,
        totals_one,
        cosine,
        sine,
        segment,
        nothing,
        0,
        [*ffn_far_sent, *ffn_near, *out_far],
    )
    out_low = links.sum_low(one_low_out, two_top_out, *out_far_sent, [rest_back])
    query_back_two, rest_back = attend_back(
        into, attended_grad, totals_two, cosine, sine, segment, rest_back, 1, out_top
    )
    into_back = jnp.concatenate([query_back_one, query_back_two, rest_back], axis=1)
    into_own, into_one_top, into_one_low, into_two_top, into_two_low, *into_far = links.corners(
        inner_rows(normed_one_all, into_back, out_low)
    )
    into_far_sent = links.sum_far(*into_far)
    into_top = links.sum_top(into_one_top, into_two_low)
    out_sent = [
        jnp.concatenate([out_top[0], out_low[0]], axis=0),
        jnp.concatenate([out_low[1], out_top[1]], axis=0),
    ]
    (normed_part,) = across(into_back, into_all, 0, (2 * rows,), into_far)
    out_sums = wide(out_own) + wide(out_sent[0]) + wide(out_sent[1])
    out_shard = links.ring_start(out_sums, weight_rows)
    out_shard = links.ring_step(out_shard, out_sums, weight_rows, 1)
    into_low = links.sum_low(
        into_one_low, into_two_top, *into_far_sent, [normed_part, *into_top]
    )
    normed_own, normed_other = part_rows(normed_part, into_far_sent)
    input_grad, _, gain_one_grad = norm_back(
        [normed_own, swap_cores(normed_other)], tokens, gain_one, hidden_grad
    )
    gains_part = jnp.concatenate([gain_one_grad, gain_two_grad], axis=0)
    gains_part = gains_part + swap_cores(gains_part)
    for step in range(2, steps):
        out_shard = links.ring_step(out_shard, out_sums, weight_rows, step)
    into_low = hold(into_low, [gains_part])
    into_sent = [
        jnp.concatenate([into_top[0], into_low[0]], axis=0),
        jnp.concatenate([into_low[1], into_top[1]], axis=0),
    ]
    into_sums = wide(into_own) + wide(into_sent[0]) + wide(into_sent[1])
    into_shard = links.ring_start(into_sums, weight_rows)
    into_shard = links.ring_step(into_shard, into_sums, weight_rows, 1)
    (gains_part,) = hold([gains_part], into_low)
    gains_level = gains_part
    for block in [links.shift(gains_part, step) for step in range(1, steps)]:
        gains_level = gains_level + block
    one_send, two_send = hold(
        [low(wide(one_low) + wide(ffn_far_sent[1])), low(wide(two_top) + wide(ffn_far_sent[0]))],
        into_low,
    )
    ffn_low = [links.swap(one_send, 1), links.swap(two_send, 2)]
    units_back = links.return_units(units_sum, ffn_low)
    for step in range(2, steps):
        if step == steps - 1:
            (into_shard,) = hold([into_shard], [gains_level, *ffn_low])
        into_shard = links.ring_step(into_shard, into_sums, weight_rows, step)
    gains_others = [links.swap(gains_level, other) for other in (1, 2, 3)]
    gains_shard = links.own_gains(gains_level + gains_others[0] + gains_others[1] + gains_others[2])
    down_shard, gate_shard, up_shard = links.join_units(units_back, 3)
    ffn_sum = jnp.concatenate(
        [
            wide(ffn_near[0]) + wide(ffn_low[1]),
            wide(ffn_low[0]) + wide(ffn_near[1]),
        ],
        axis=0,
    )
    activations = low(hidden_state + (wide(ffn_own) + ffn_sum))
    query_shard = into_shard[:, :query_cols]
    key_shard = into_shard[:, query_cols : query_cols + key_cols]
    value_shard = into_shard[:, query_cols + key_cols :]
    q_all = adam(query_weight, query_shard, query_moment, query_square, RATE_MAIN, DECAY_RATE)
    k_all = adam(key_weight, key_shard, key_moment, key_square, RATE_MAIN, DECAY_RATE)
    v_all = adam(value_weight, value_shard, value_moment, value_square, RATE_MAIN, DECAY_RATE)
    o_all = adam(out_weight, out_shard, out_moment, out_square, RATE_OUT, DECAY_RATE)
    g_all = adam(gate_weight, gate_shard, gate_moment, gate_square, RATE_MAIN, DECAY_RATE)
    u_all = adam(up_weight, up_shard, up_moment, up_square, RATE_MAIN, DECAY_RATE)
    d_all = adam(down_weight, down_shard, down_moment, down_square, RATE_DOWN, DECAY_RATE)
    n_all = adam(norm_gains, gains_shard, gains_moment, gains_square, RATE_GAINS, 0.0)
    return (
        activations,
        input_grad,
        q_all[0],
        q_all[1],
        q_all[2],
        q_all[3],
        k_all[0],
        k_all[1],
        k_all[2],
        k_all[3],
        v_all[0],
        v_all[1],
        v_all[2],
        v_all[3],
        o_all[0],
        o_all[1],
        o_all[2],
        o_all[3],
        g_all[0],
        g_all[1],
        g_all[2],
        g_all[3],
        u_all[0],
        u_all[1],
        u_all[2],
        u_all[3],
        d_all[0],
        d_all[1],
        d_all[2],
        d_all[3],
        n_all[0],
        n_all[1],
        n_all[2],
        n_all[3],
    )


def solution(mesh):
    in_specs = (
        P(("dp", "tensor"), None),
        P(("dp", "tensor"), None),
        P("dp", None),
        P("dp", "tensor"),
        P("dp", "tensor"),
        P("dp", "tensor"),
        P("dp", "tensor"),
        P("dp", "tensor"),
        P("dp", "tensor"),
        P("dp", "tensor"),
        P(None, "dp"),
        P("dp", "tensor"),
        P("dp", "tensor"),
        P("dp", "tensor"),
        P("dp", "tensor"),
        P("dp", "tensor"),
        P("dp", "tensor"),
        P("dp", "tensor"),
        P(None, "dp"),
        P("dp", "tensor"),
        P("dp", "tensor"),
        P("dp", "tensor"),
        P("dp", "tensor"),
        P("dp", "tensor"),
        P("dp", "tensor"),
        P("dp", "tensor"),
        P(None, "dp"),
    )
    out_specs = (
        P(("dp", "tensor"), None),
        P(("dp", "tensor"), None),
        P("dp", "tensor"),
        P("dp", "tensor"),
        P("dp", "tensor"),
        P("dp", "tensor"),
        P("dp", "tensor"),
        P("dp", "tensor"),
        P("dp", "tensor"),
        P("dp", "tensor"),
        P("dp", "tensor"),
        P("dp", "tensor"),
        P("dp", "tensor"),
        P("dp", "tensor"),
        P("dp", "tensor"),
        P("dp", "tensor"),
        P("dp", "tensor"),
        P("dp", "tensor"),
        P("dp", "tensor"),
        P("dp", "tensor"),
        P("dp", "tensor"),
        P("dp", "tensor"),
        P("dp", "tensor"),
        P("dp", "tensor"),
        P("dp", "tensor"),
        P("dp", "tensor"),
        P("dp", "tensor"),
        P("dp", "tensor"),
        P("dp", "tensor"),
        P("dp", "tensor"),
        P(None, "dp"),
        P(None, "dp"),
        P(None, "dp"),
        P(None, "dp"),
    )
    links = Links(mesh.shape["dp"])
    return jax.shard_map(functools.partial(shards, links), mesh=mesh, in_specs=in_specs, out_specs=out_specs, check_vma=False)
```

```python
import functools
import math

import jax
import jax.numpy as jnp
from jax import lax
from jax.experimental import pallas as pl
from jax.experimental.pallas import tpu as pltpu
from jax.sharding import PartitionSpec as P

HEAD = 64
STEP = 10


NORM_EPS = 1e-05
NEG_LARGE = -1000000000.0
BETA_FIRST = 0.9
BETA_SECOND = 0.95
ADAM_EPS = 1e-08
DECAY_RATE = 0.1
RATE_MAIN = 0.02
RATE_OUT = 0.15
RATE_DOWN = 0.015
RATE_GAINS = 0.6


def rope_tables(segment):
    length = segment.shape[0]
    order = jnp.arange(length, dtype=jnp.int32)
    before = jnp.sum((segment[None, :] < segment[:, None]).astype(jnp.int32), axis=1)
    place = (order - before).astype(jnp.float32)
    half = HEAD // 2
    freq = jnp.exp(jnp.arange(half, dtype=jnp.float32) * (-2.0 * math.log(10000.0) / HEAD))
    angle = place[:, None] * freq[None, :]
    cosine, sine = jnp.cos(angle), jnp.sin(angle)
    return (
        jnp.concatenate([cosine] * 4, axis=1),
        jnp.concatenate([-sine, sine, -sine, sine], axis=1),
    )


def contract_rows(left, right):
    return lax.dot_general(
        left, right, (((0,), (0,)), ((), ())), preferred_element_type=jnp.float32
    )


def contract_cols(left, right):
    return lax.dot_general(
        left, right, (((1,), (1,)), ((), ())), preferred_element_type=jnp.float32
    )


def adam(weight, grad, moment, square, rate, decay):
    moment_new = BETA_FIRST * moment + (1.0 - BETA_FIRST) * grad
    square_new = BETA_SECOND * square + (1.0 - BETA_SECOND) * grad * grad
    direction = (
        moment_new
        / (1.0 - BETA_FIRST**STEP)
        / (jnp.sqrt(square_new / (1.0 - BETA_SECOND**STEP)) + ADAM_EPS)
    )
    return (grad, moment_new, square_new, weight - rate * (direction + decay * weight))


LOW = jnp.bfloat16
PLANE = 4
LANES = 128
TILE = 256
ROWS = 384
VMEM_LIMIT = 48 * 1024 * 1024
SMALL_COST = pl.CostEstimate(flops=1024, bytes_accessed=1024, transcendentals=0)
LARGE_COST = pl.CostEstimate(flops=1 << 35, bytes_accessed=1 << 20, transcendentals=0)


def swap_cores(block):
    return lax.ppermute(block, "tensor", [(0, 1), (1, 0)])


def late(kernel, count, *refs):
    ins, rest = refs[: count[0]], refs[count[0] + count[1] :]
    kernel(*ins, *rest)


def call(kernel, waits, operands, *, in_specs, cost=LARGE_COST, **options):
    place = pl.BlockSpec(memory_space=pltpu.HBM)
    return pl.pallas_call(
        functools.partial(late, kernel, (len(operands), len(waits))),
        in_specs=list(in_specs) + [place] * len(waits),
        compiler_params=pltpu.CompilerParams(vmem_limit_bytes=VMEM_LIMIT),
        cost_estimate=cost,
        **options,
    )(*operands, *waits)


def lane_of(shape):
    return lax.broadcasted_iota(jnp.int32, shape, len(shape) - 1)


def turn_heads(values, cosine, sine):
    first = lane_of(values.shape) % HEAD < HEAD // 2
    ahead = pltpu.roll(values, LANES - HEAD // 2, 1)
    behind = pltpu.roll(values, HEAD // 2, 1)
    return values * cosine + jnp.where(first, ahead, behind) * sine


def project_kernel(heads, normed_ref, weight_ref, cosine_ref, sine_ref, out_ref):
    part = jnp.dot(normed_ref[...], weight_ref[...], preferred_element_type=jnp.float32)
    cosine, sine = cosine_ref[...], sine_ref[...]
    step = pl.program_id(0)
    for at in range(0, part.shape[1], LANES):
        piece = part[:, at : at + LANES]
        turned = turn_heads(piece, cosine, sine)
        keep = step * part.shape[1] + at >= heads
        out_ref[:, at : at + LANES] = jnp.where(keep, piece, turned).astype(LOW)


def project(normed, weight, cosine, sine, turned, waits=()):
    rows, depth = normed.shape
    columns = weight.shape[1]
    block = 2 * LANES
    return call(
        functools.partial(project_kernel, turned),
        waits,
        (normed, weight, cosine, sine),
        cost=SMALL_COST,
        grid=(columns // block,),
        in_specs=[
            pl.BlockSpec((rows, depth), lambda i: (0, 0)),
            pl.BlockSpec((depth, block), lambda i: (0, i)),
            pl.BlockSpec((rows, LANES), lambda i: (0, 0)),
            pl.BlockSpec((rows, LANES), lambda i: (0, 0)),
        ],
        out_specs=pl.BlockSpec((rows, block), lambda i: (0, i)),
        out_shape=jax.ShapeDtypeStruct((rows, columns), LOW),
    )


def double(values, group):
    low_half = lane_of(values.shape) < HEAD
    other = pltpu.roll(values.astype(jnp.float32), HEAD, 1).astype(values.dtype)
    return jnp.where(low_half == (group == 0), values, other)


def set_bias(across_ref, down_ref, bias):
    rows = bias.shape[0]
    row = lax.broadcasted_iota(jnp.int32, (rows, rows), 0)
    column = lax.broadcasted_iota(jnp.int32, (rows, rows), 1)
    allowed = (down_ref[...] == across_ref[...]) & (column <= row)
    bias[...] = jnp.where(allowed, 0.0, NEG_LARGE)


def halves_of(block):
    low_half = lane_of(block.shape) < HEAD
    zero = jnp.zeros_like(block)
    return jnp.where(low_half, block, zero), jnp.where(low_half, zero, block)


def dot_last(left, right):
    return lax.dot_general(
        left, right, (((1,), (1,)), ((), ())), preferred_element_type=jnp.float32
    )


def dot_first(left, right):
    return lax.dot_general(
        left, right, (((0,), (0,)), ((), ())), preferred_element_type=jnp.float32
    )


def attend_kernel(
    group, query_ref, key_ref, value_ref, across_ref, down_ref, out_ref, total_ref, bias, keys, values
):
    step = pl.program_id(0)
    rows = query_ref.shape[0]

    @pl.when(step == 0)
    def _():
        set_bias(across_ref, down_ref, bias)
        total_ref[...] = jnp.zeros_like(total_ref)
        keys[...] = double(key_ref[...], group)
        values[...] = double(value_ref[...], group)

    for start in range(0, rows, TILE):
        stop = start + TILE
        query = query_ref[start:stop, :] * jnp.asarray(HEAD**-0.5, LOW)
        key, value = keys[:stop, :], values[:stop, :]
        shade = bias[start:stop, :stop]
        outs = []
        lane = lane_of((TILE, LANES))
        totals = total_ref[start:stop, :]
        for side, part in enumerate(halves_of(query)):
            score = dot_last(part, key) + shade
            largest = jnp.max(score, axis=1, keepdims=True)
            expo = jnp.exp(score - largest)
            total = jnp.sum(expo, axis=1, keepdims=True)
            probs = (expo * (1.0 / total)).astype(LOW)
            outs.append(jnp.dot(probs, value, preferred_element_type=jnp.float32))
            totals = jnp.where(lane == 2 * step + side, largest + jnp.log(total), totals)
        total_ref[start:stop, :] = totals
        out_ref[start:stop, :] = jnp.where(lane < HEAD, outs[0], outs[1]).astype(LOW)


def attend(into, segment, query_cols, group, waits=()):
    rows = into.shape[0]
    pairs = query_cols // LANES
    here = pairs // 2
    return call(
        functools.partial(attend_kernel, group),
        waits,
        (into, into, into, segment[None, :], segment[:, None]),
        cost=SMALL_COST,
        grid=(here,),
        in_specs=[
            pl.BlockSpec((rows, LANES), lambda i: (0, group * here + i)),
            pl.BlockSpec((rows, LANES), lambda i: (0, pairs)),
            pl.BlockSpec((rows, LANES), lambda i: (0, pairs + 1)),
            pl.BlockSpec((1, rows), lambda i: (0, 0)),
            pl.BlockSpec((rows, 1), lambda i: (0, 0)),
        ],
        out_specs=[
            pl.BlockSpec((rows, LANES), lambda i: (0, i)),
            pl.BlockSpec((rows, LANES), lambda i: (0, 0)),
        ],
        out_shape=[
            jax.ShapeDtypeStruct((rows, query_cols // 2), LOW),
            jax.ShapeDtypeStruct((rows, LANES), jnp.float32),
        ],
        scratch_shapes=[
            pltpu.VMEM((rows, rows), jnp.float32),
            pltpu.VMEM((rows, LANES), LOW),
            pltpu.VMEM((rows, LANES), LOW),
        ],
    )


def attend_back_kernel(
    group,
    query_ref,
    key_ref,
    value_ref,
    upstream_ref,
    total_ref,
    cosine_ref,
    sine_ref,
    across_ref,
    down_ref,
    before_ref,
    query_back_ref,
    rest_ref,
    bias,
    keys,
    values,
    key_sum,
    value_sum,
):
    step = pl.program_id(0)
    rows = query_ref.shape[0]

    @pl.when(step == 0)
    def _():
        set_bias(across_ref, down_ref, bias)
        keys[...] = double(key_ref[...], group)
        values[...] = double(value_ref[...], group)
        key_sum[...] = jnp.zeros_like(key_sum)
        value_sum[...] = jnp.zeros_like(value_sum)

    scale = jnp.asarray(HEAD**-0.5, LOW)
    for start in range(0, rows, TILE):
        stop = start + TILE
        query = query_ref[start:stop, :] * scale
        upstream = upstream_ref[start:stop, :]
        key, value = keys[:stop, :], values[:stop, :]
        shade = bias[start:stop, :stop]
        lane = lane_of((TILE, LANES))
        backs = []
        key_part = value_part = None
        for side, (part, grad) in enumerate(zip(halves_of(query), halves_of(upstream))):
            log_total = jnp.sum(
                jnp.where(lane == 2 * step + side, total_ref[start:stop, :], 0.0),
                axis=1,
                keepdims=True,
            )
            probs = jnp.exp(dot_last(part, key) + shade - log_total)
            value_here = dot_first(probs.astype(LOW), grad)
            probs_grad = dot_last(grad, value)
            delta = jnp.sum(probs * probs_grad, axis=1, keepdims=True)
            score_grad = (probs * (probs_grad - delta)).astype(LOW)
            backs.append(jnp.dot(score_grad, key, preferred_element_type=jnp.float32))
            key_here = dot_first(score_grad, part)
            key_part = key_here if key_part is None else key_part + key_here
            value_part = value_here if value_part is None else value_part + value_here
        key_sum[:stop, :] += key_part
        value_sum[:stop, :] += value_part
        back = jnp.where(lane < HEAD, backs[0], backs[1]) * HEAD**-0.5
        back = turn_heads(back, cosine_ref[start:stop, :], -sine_ref[start:stop, :])
        query_back_ref[start:stop, :] = back.astype(LOW)

    @pl.when(step == pl.num_programs(0) - 1)
    def _():
        key_back = key_sum[...] + pltpu.roll(key_sum[...], HEAD, 1)
        key_back = turn_heads(key_back, cosine_ref[...], -sine_ref[...]).astype(LOW)
        value_back = (value_sum[...] + pltpu.roll(value_sum[...], HEAD, 1)).astype(LOW)
        first = (lane_of(key_back.shape) < HEAD) & (group > 0)
        rest_ref[:, :LANES] = jnp.where(first, before_ref[:, :LANES], key_back)
        rest_ref[:, LANES:] = jnp.where(first, before_ref[:, LANES:], value_back)


def attend_back(into, upstream, log_totals, cosine, sine, segment, before, group, waits=()):
    rows, query_cols = upstream.shape
    pairs = query_cols // LANES
    here = pairs // 2
    whole = lambda width: pl.BlockSpec((rows, width), lambda i: (0, 0))
    return call(
        functools.partial(attend_back_kernel, group),
        waits,
        (into, into, into, upstream, log_totals, cosine, sine, segment[None, :], segment[:, None], before),
        grid=(here,),
        in_specs=[
            pl.BlockSpec((rows, LANES), lambda i: (0, group * here + i)),
            pl.BlockSpec((rows, LANES), lambda i: (0, pairs)),
            pl.BlockSpec((rows, LANES), lambda i: (0, pairs + 1)),
            pl.BlockSpec((rows, LANES), lambda i: (0, group * here + i)),
            whole(LANES),
            whole(LANES),
            whole(LANES),
            pl.BlockSpec((1, rows), lambda i: (0, 0)),
            whole(1),
            whole(2 * LANES),
        ],
        out_specs=[pl.BlockSpec((rows, LANES), lambda i: (0, i)), whole(2 * LANES)],
        out_shape=[
            jax.ShapeDtypeStruct((rows, query_cols // 2), LOW),
            jax.ShapeDtypeStruct((rows, 2 * LANES), LOW),
        ],
        scratch_shapes=[
            pltpu.VMEM((rows, rows), jnp.float32),
            pltpu.VMEM((rows, LANES), LOW),
            pltpu.VMEM((rows, LANES), LOW),
            pltpu.VMEM((rows, LANES), jnp.float32),
            pltpu.VMEM((rows, LANES), jnp.float32),
        ],
    )


def across_kernel(cuts, left_ref, right_ref, *out_refs):
    part = dot_last(left_ref[...], right_ref[...]).astype(LOW)
    start = 0
    for rows, out_ref in zip(cuts, out_refs):
        out_ref[...] = part[start : start + rows]
        start += rows


def across(left, right, first, cuts, waits=()):
    depth, columns = right.shape[1], right.shape[0]
    rows = sum(cuts)
    block = min(columns, 4 * LANES)
    assert first % rows == 0
    return call(
        functools.partial(across_kernel, cuts),
        waits,
        (left, right),
        grid=(columns // block,),
        in_specs=[
            pl.BlockSpec((rows, depth), lambda i: (first // rows, 0)),
            pl.BlockSpec((block, depth), lambda i: (i, 0)),
        ],
        out_specs=[pl.BlockSpec((cut, block), lambda i: (0, i)) for cut in cuts],
        out_shape=[jax.ShapeDtypeStruct((cut, columns), LOW) for cut in cuts],
    )


def plain_kernel(left_ref, right_ref, out_ref):
    out_ref[...] = jnp.dot(
        left_ref[...], right_ref[...], preferred_element_type=jnp.float32
    ).astype(LOW)


def plain(left, right, waits=()):
    rows, depth = left.shape
    columns = right.shape[1]
    block = 2 * LANES
    return call(
        plain_kernel,
        waits,
        (left, right),
        grid=(columns // block,),
        in_specs=[
            pl.BlockSpec((rows, depth), lambda i: (0, 0)),
            pl.BlockSpec((depth, block), lambda i: (0, i)),
        ],
        out_specs=pl.BlockSpec((rows, block), lambda i: (0, i)),
        out_shape=jax.ShapeDtypeStruct((rows, columns), LOW),
    )


def join_kernel(first_ref, second_ref, far_one_ref, far_two_ref, one_ref, two_ref):
    half = far_one_ref.shape[0]
    one_ref[:half] = first_ref[:half]
    one_ref[half:] = low(wide(first_ref[half:]) + wide(far_two_ref[...]))
    two_ref[:half] = low(wide(second_ref[:half]) + wide(far_one_ref[...]))
    two_ref[half:] = second_ref[half:]


def join_sends(first, second, far_one, far_two, waits=()):
    rows, columns = first.shape
    block = min(columns, 4 * LANES) if columns % (4 * LANES) == 0 else 2 * LANES
    full = pl.BlockSpec((rows, block), lambda i: (0, i))
    part = pl.BlockSpec((rows // 2, block), lambda i: (0, i))
    shape = jax.ShapeDtypeStruct((rows, columns), LOW)
    return call(
        join_kernel,
        waits,
        (first, second, far_one, far_two),
        cost=SMALL_COST,
        grid=(columns // block,),
        in_specs=[full, full, part, part],
        out_specs=[full, full],
        out_shape=[shape, shape],
    )


def norm_back_kernel(count, *refs):
    grads = refs[:count]
    values_ref, gain_ref, plus_ref, sum_ref, low_ref, gain_grad_ref = refs[count:]
    grad = sum(wide(ref[...]) for ref in grads)
    values = wide(values_ref[...])
    mean = jnp.mean(values * values, axis=1, keepdims=True)
    inverse = lax.rsqrt(mean + NORM_EPS)
    weighted = gain_ref[...] * grad
    across_mean = jnp.mean(weighted * values, axis=1, keepdims=True)
    back = inverse * weighted - values * (inverse * inverse * inverse) * across_mean
    total = wide(plus_ref[...]) + back
    sum_ref[...] = total
    low_ref[...] = low(total)

    @pl.when(pl.program_id(0) == 0)
    def _():
        gain_grad_ref[...] = jnp.zeros_like(gain_grad_ref)

    gain_grad_ref[...] += jnp.sum(grad * values * inverse, axis=0, keepdims=True)


def norm_back(grads, values, gain, plus, waits=()):
    rows, columns = values.shape
    block = LANES
    row = by_rows(block, columns)
    line = pl.BlockSpec((1, columns), lambda i: (0, 0))
    return call(
        functools.partial(norm_back_kernel, len(grads)),
        waits,
        (*grads, values, gain[None, :], plus),
        cost=SMALL_COST,
        grid=(rows // block,),
        in_specs=[row] * len(grads) + [row, line, row],
        out_specs=[row, row, line],
        out_shape=[
            jax.ShapeDtypeStruct((rows, columns), jnp.float32),
            jax.ShapeDtypeStruct((rows, columns), LOW),
            jax.ShapeDtypeStruct((1, columns), jnp.float32),
        ],
    )


def gate_up_kernel(normed_ref, weight_ref, out_ref):
    out_ref[...] = jnp.dot(normed_ref[...], weight_ref[...], preferred_element_type=jnp.float32)


def hidden_kernel(upstream_ref, down_ref, gate_up_ref, inner_ref, grads_ref):
    width = down_ref.shape[1]
    grad = jnp.dot(upstream_ref[...], down_ref[...], preferred_element_type=jnp.float32)
    gate = gate_up_ref[:, :width]
    upper = gate_up_ref[:, width:]
    sigma = 1.0 / (1.0 + jnp.exp(-gate))
    active = gate * sigma
    inner_ref[...] = (active * upper).astype(LOW)
    slope = sigma * (1.0 + gate * (1.0 - sigma))
    grads_ref[:, :width] = (grad * upper * slope).astype(LOW)
    grads_ref[:, width:] = (grad * active).astype(LOW)


def held(array):
    return pl.BlockSpec(array.shape, lambda i: (0, 0), pipeline_mode=pl.Buffered(1))


def by_rows(block, width):
    return pl.BlockSpec((block, width), lambda i: (i, 0))


def gate_and_up(normed, weight, waits=()):
    rows, depth = normed.shape
    columns = weight.shape[1]
    return call(
        gate_up_kernel,
        waits,
        (normed, weight),
        grid=(rows // ROWS,),
        in_specs=[by_rows(ROWS, depth), held(weight)],
        out_specs=by_rows(ROWS, columns),
        out_shape=jax.ShapeDtypeStruct((rows, columns), jnp.float32),
    )


def hidden(upstream, down, gate_up, waits=()):
    rows, depth = upstream.shape
    width = down.shape[1]
    return call(
        hidden_kernel,
        waits,
        (upstream, down, gate_up),
        grid=(rows // ROWS,),
        in_specs=[by_rows(ROWS, depth), held(down), by_rows(ROWS, 2 * width)],
        out_specs=[by_rows(ROWS, width), by_rows(ROWS, 2 * width)],
        out_shape=[
            jax.ShapeDtypeStruct((rows, width), LOW),
            jax.ShapeDtypeStruct((rows, 2 * width), LOW),
        ],
    )


def inner_kernel(left_ref, right_ref, out_ref):
    out_ref[...] = dot_first(left_ref[...], right_ref[...]).astype(LOW)


def inner_rows(left, right, waits=()):
    depth, rows = left.shape
    columns = right.shape[1]
    block = 2 * LANES
    return call(
        inner_kernel,
        waits,
        (left, right),
        grid=(rows // block,),
        in_specs=[pl.BlockSpec((depth, block), lambda i: (0, i)), held(right)],
        out_specs=pl.BlockSpec((block, columns), lambda i: (i, 0)),
        out_shape=jax.ShapeDtypeStruct((rows, columns), LOW),
    )


def put_halves(core_ref, part, keep_ref, give_ref):
    rows = keep_ref.shape[1]
    first = core_ref[0] == 0
    for at in range(keep_ref.shape[0]):
        start = 2 * rows * at
        top, bottom = part[start : start + rows], part[start + rows : start + 2 * rows]
        keep_ref[at] = jnp.where(first, top, bottom)
        give_ref[at] = jnp.where(first, bottom, top)


def unit_grads_kernel(blocks, count, core_ref, *refs):
    upstream, inner, normed, grads = [refs[at * count : (at + 1) * count] for at in range(4)]
    down_keep_ref, down_give_ref, keep_ref, give_ref = refs[4 * count :]
    step = pl.program_id(0)

    @pl.when(step < blocks)
    def _():
        part = sum(dot_first(one[...], two[...]) for one, two in zip(upstream, inner))
        put_halves(core_ref, low(part), down_keep_ref, down_give_ref)

    @pl.when(step >= blocks)
    def _():
        part = sum(dot_first(one[...], two[...]) for one, two in zip(normed, grads))
        put_halves(core_ref, low(part), keep_ref, give_ref)


def unit_grads(upstream, inner, normed, grads, rows, waits=()):
    total = upstream[0].shape[1]
    block = 2 * LANES
    blocks, lots = total // block, block // rows // 2
    core = lax.axis_index("tensor").astype(jnp.int32).reshape(1)
    early = lambda i: jnp.minimum(i, blocks - 1)
    late_on = lambda i: jnp.maximum(i - blocks, 0)
    out = lambda width, when: pl.BlockSpec((lots, rows, width), lambda i: (when(i), 0, 0))
    shape = lambda width: jax.ShapeDtypeStruct((total // rows // 2, rows, width), LOW)
    left = lambda array, when: pl.BlockSpec((array.shape[0], block), lambda i: (0, when(i)))
    widths = inner[0].shape[1], grads[0].shape[1]
    return call(
        functools.partial(unit_grads_kernel, blocks, len(upstream)),
        waits,
        (core, *upstream, *inner, *normed, *grads),
        grid=(2 * blocks,),
        in_specs=[
            pl.BlockSpec(memory_space=pltpu.SMEM),
            *[left(array, early) for array in upstream],
            *[held(array) for array in inner],
            *[left(array, late_on) for array in normed],
            *[held(array) for array in grads],
        ],
        out_specs=[out(widths[0], early)] * 2 + [out(widths[1], late_on)] * 2,
        out_shape=[shape(widths[0])] * 2 + [shape(widths[1])] * 2,
    )


def hold_kernel(*refs):
    half = len(refs) // 2
    for source, target in zip(refs[:half], refs[half:]):
        target[...] = source[...]


def hold(values, waits=()):
    specs = [pl.BlockSpec(value.shape, lambda *_, rank=value.ndim: (0,) * rank) for value in values]
    return list(
        call(
            hold_kernel,
            waits,
            values,
            cost=SMALL_COST,
            grid=(1,),
            in_specs=specs,
            out_specs=specs,
            out_shape=[jax.ShapeDtypeStruct(value.shape, value.dtype) for value in values],
        )
    )


def nothing_kernel(*refs):
    del refs


def fence(values, waits=()):
    place = pl.BlockSpec(memory_space=pltpu.HBM)
    return list(
        pl.pallas_call(
            nothing_kernel,
            in_specs=[place] * (len(values) + len(waits)),
            out_specs=[place] * len(values),
            out_shape=[jax.ShapeDtypeStruct(value.shape, value.dtype) for value in values],
            input_output_aliases={at: at for at in range(len(values))},
            compiler_params=pltpu.CompilerParams(vmem_limit_bytes=1024 * 1024),
            cost_estimate=SMALL_COST,
        )(*values, *waits)
    )


def move_kernel(counts, cuts, extra, spots_ref, *refs):
    *blocks, sems = refs
    sources, targets = blocks[: len(counts)], blocks[len(counts) + extra :]
    copies, step = [], 0
    for count, source in zip(counts, sources):
        for at in range(count):
            for (left, right), target in zip(cuts, targets):
                part = source.at[at] if len(cuts) == 1 else source.at[at, :, left:right]
                copies.append(
                    pltpu.make_async_copy(part, target.at[spots_ref[step]], sems.at[len(copies)])
                )
            step += 1
    for copy in copies:
        copy.start()
    for copy in copies:
        copy.wait()


def move(blocks, spots, cuts=None, waits=()):
    counts = [block.shape[0] for block in blocks]
    rows, columns = blocks[0].shape[1:]
    ends = [0, *(cuts or []), columns]
    lots = list(zip(ends[:-1], ends[1:]))
    place = pl.BlockSpec(memory_space=pltpu.HBM)
    return pl.pallas_call(
        functools.partial(move_kernel, counts, lots, len(waits)),
        in_specs=[pl.BlockSpec(memory_space=pltpu.SMEM)] + [place] * (len(blocks) + len(waits)),
        out_specs=[place] * len(lots),
        out_shape=[
            jax.ShapeDtypeStruct((sum(counts), rows, right - left), LOW) for left, right in lots
        ],
        scratch_shapes=[pltpu.SemaphoreType.DMA((sum(counts) * len(lots),))],
        compiler_params=pltpu.CompilerParams(vmem_limit_bytes=1024 * 1024),
        cost_estimate=SMALL_COST,
    )(spots, *blocks, *waits)


def split_kernel(left_columns, whole_ref, left_ref, right_ref):
    left_ref[...] = whole_ref[:, :, :left_columns]
    right_ref[...] = whole_ref[:, :, left_columns:]


def split_columns(whole, left, waits=()):
    lots, rows, columns = whole.shape
    block = max(1, lots // 4)
    spec = lambda width: pl.BlockSpec((block, rows, width), lambda i: (i, 0, 0))
    shape = lambda width: jax.ShapeDtypeStruct((lots, rows, width), LOW)
    return call(
        functools.partial(split_kernel, left),
        waits,
        (whole,),
        cost=SMALL_COST,
        grid=(lots // block,),
        in_specs=[spec(columns)],
        out_specs=[spec(left), spec(columns - left)],
        out_shape=[shape(left), shape(columns - left)],
    )


def spread_kernel(cuts, extra, spots_ref, own_ref, other_ref, *refs):
    *targets, sems = refs[extra:]
    copies = []
    for at, source in enumerate((own_ref, other_ref)):
        for (left, right), target in zip(cuts, targets):
            copies.append(
                pltpu.make_async_copy(
                    source.at[:, :, left:right], target.at[:, spots_ref[at]], sems.at[len(copies)]
                )
            )
    for copy in copies:
        copy.start()
    for copy in copies:
        copy.wait()


def spread_halves(own, other, spots, cuts):
    count, rows, columns = own.shape
    ends = [0, *cuts, columns]
    lots = list(zip(ends[:-1], ends[1:]))
    place = pl.BlockSpec(memory_space=pltpu.HBM)
    return pl.pallas_call(
        functools.partial(spread_kernel, lots, 0),
        in_specs=[pl.BlockSpec(memory_space=pltpu.SMEM), place, place],
        out_specs=[place] * len(lots),
        out_shape=[
            jax.ShapeDtypeStruct((count, 2, rows, right - left), LOW) for left, right in lots
        ],
        scratch_shapes=[pltpu.SemaphoreType.DMA((2 * len(lots),))],
        compiler_params=pltpu.CompilerParams(vmem_limit_bytes=1024 * 1024),
        cost_estimate=SMALL_COST,
    )(spots, own, other)


def pick_kernel(count, spots_ref, *refs):
    del spots_ref
    for source, target in zip(refs[:count], refs[len(refs) - count :]):
        target[...] = source[0]


def pick(parts, spots, waits=()):
    lots, _, rows, columns = parts.shape
    count = spots.shape[0]
    place = pl.BlockSpec(memory_space=pltpu.HBM)
    return pl.pallas_call(
        functools.partial(pick_kernel, count),
        grid_spec=pltpu.PrefetchScalarGridSpec(
            num_scalar_prefetch=1,
            grid=(lots,),
            in_specs=[
                pl.BlockSpec(
                    (1, 1, rows, columns), lambda i, spots_ref, at=at: (i, spots_ref[at], 0, 0)
                )
                for at in range(count)
            ]
            + [place] * len(waits),
            out_specs=[
                pl.BlockSpec((1, rows, columns), lambda i, spots_ref: (i, 0, 0))
                for at in range(count)
            ],
        ),
        out_shape=[jax.ShapeDtypeStruct((lots, rows, columns), LOW)] * count,
        compiler_params=pltpu.CompilerParams(vmem_limit_bytes=VMEM_LIMIT),
        cost_estimate=SMALL_COST,
    )(spots, *[parts] * count, *waits)


def add_kernel(*refs):
    out_ref = refs[-1]
    start = 0
    for one_ref, two_ref in zip(refs[:-1:2], refs[1:-1:2]):
        stop = start + one_ref.shape[2]
        out_ref[:, :, start:stop] = low(wide(one_ref[...]) + wide(two_ref[...]))
        start = stop


def add_low(pairs, waits=()):
    lots, rows, _ = pairs[0][0].shape
    block = max(1, lots // 4)
    spec = lambda width: pl.BlockSpec((block, rows, width), lambda i: (i, 0, 0))
    arrays = [array for pair in pairs for array in pair]
    total = sum(one.shape[2] for one, _ in pairs)
    return call(
        add_kernel,
        waits,
        arrays,
        cost=SMALL_COST,
        grid=(lots // block,),
        in_specs=[spec(array.shape[2]) for array in arrays],
        out_specs=spec(total),
        out_shape=jax.ShapeDtypeStruct((lots, rows, total), LOW),
    )


def norm_kernel(values_ref, gain_ref, out_ref):
    values = wide(values_ref[...])
    mean = jnp.mean(values * values, axis=1, keepdims=True)
    out_ref[...] = low(values * lax.rsqrt(mean + NORM_EPS) * gain_ref[...])


def norm(values, gain, waits=()):
    rows, columns = values.shape
    row = by_rows(LANES, columns)
    return call(
        norm_kernel,
        waits,
        (values, gain[None, :]),
        cost=SMALL_COST,
        grid=(rows // LANES,),
        in_specs=[row, pl.BlockSpec((1, columns), lambda i: (0, 0))],
        out_specs=row,
        out_shape=jax.ShapeDtypeStruct((rows, columns), LOW),
    )


def order_rows(own, other):
    core = lax.axis_index("tensor").astype(jnp.int32)
    (whole,) = move([own[None], other[None]], jnp.stack([core, 1 - core]))
    return whole.reshape(-1, own.shape[1])


def pick_halves_kernel(count, half, spots_ref, *refs):
    del spots_ref
    targets = refs[count:]
    step = pl.program_id(0)
    targets[0][...] = refs[0][0]

    @pl.when(step < half)
    def _():
        for at in range(1, count):
            targets[2 * at - 1][...] = refs[at][0]

    @pl.when(step >= half)
    def _():
        for at in range(1, count):
            targets[2 * at][...] = refs[at][0]


def pick_halves(parts, spots):
    lots, _, rows, columns = parts.shape
    count, half = spots.shape[0], lots // 2
    spec = lambda where: pl.BlockSpec((1, rows, columns), where)
    shape = lambda size: jax.ShapeDtypeStruct((size, rows, columns), LOW)
    early = spec(lambda i, spots_ref: (jnp.minimum(i, half - 1), 0, 0))
    late_on = spec(lambda i, spots_ref: (jnp.maximum(i - half, 0), 0, 0))
    found = pl.pallas_call(
        functools.partial(pick_halves_kernel, count, half),
        grid_spec=pltpu.PrefetchScalarGridSpec(
            num_scalar_prefetch=1,
            grid=(lots,),
            in_specs=[
                pl.BlockSpec(
                    (1, 1, rows, columns), lambda i, spots_ref, at=at: (i, spots_ref[at], 0, 0)
                )
                for at in range(count)
            ],
            out_specs=[spec(lambda i, spots_ref: (i, 0, 0))] + [early, late_on] * (count - 1),
        ),
        out_shape=[shape(lots)] + [shape(half), shape(lots - half)] * (count - 1),
        compiler_params=pltpu.CompilerParams(vmem_limit_bytes=VMEM_LIMIT),
        cost_estimate=SMALL_COST,
    )(spots, *[parts] * count)
    return [block.reshape(-1, columns) for block in found]


def add_pairs_kernel(*refs):
    third = len(refs) // 3
    for one_ref, two_ref, out_ref in zip(refs[:third], refs[third : 2 * third], refs[2 * third :]):
        out_ref[...] = low(wide(one_ref[...]) + wide(two_ref[...]))


def add_pairs(ones, twos, waits=()):
    rows, columns = ones[0].shape
    block = columns // 2
    spec = pl.BlockSpec((rows, block), lambda i: (0, i))
    return call(
        add_pairs_kernel,
        waits,
        (*ones, *twos),
        cost=SMALL_COST,
        grid=(2,),
        in_specs=[spec] * (2 * len(ones)),
        out_specs=[spec] * len(ones),
        out_shape=[jax.ShapeDtypeStruct((rows, columns), LOW)] * len(ones),
    )


def part_rows(whole, waits=()):
    core = lax.axis_index("tensor").astype(jnp.int32)
    rows, columns = whole.shape[0] // 2, whole.shape[1]
    own, other = pick(whole.reshape(1, 2, rows, columns), jnp.stack([core, 1 - core]), waits)
    return own[0], other[0]


def wide(block):
    return block.astype(jnp.float32)


def low(block):
    return block.astype(LOW)


def order_cores(own, other, axis=0):
    return jnp.where(
        lax.axis_index("tensor") == 0,
        jnp.concatenate([own, other], axis=axis),
        jnp.concatenate([other, own], axis=axis),
    )


class Links:
    def __init__(self, devices):
        self.devices = devices
        self.planes = devices // PLANE
        self.pairs = {
            step: [(index, index ^ step) for index in range(devices)] for step in (1, 2, 3)
        }
        self.columns = [list(range(corner, devices, PLANE)) for corner in range(PLANE)]
        self.ring = [(index, (index + PLANE) % devices) for index in range(devices)]

    def swap(self, block, step):
        return lax.ppermute(block, "dp", self.pairs[step])

    def turn(self, block):
        return lax.ppermute(block, "dp", self.ring)

    def place(self):
        index = lax.axis_index("dp").astype(jnp.int32)
        return index // PLANE, index % PLANE

    def corner_spots(self):
        _, corner = self.place()
        return jnp.stack([corner ^ other for other in range(PLANE)])

    def shift(self, block, step):
        pairs = [(at, (at + PLANE * step) % self.devices) for at in range(self.devices)]
        return lax.ppermute(block, "dp", pairs)

    def gather_near(self, block):
        return [self.swap(block, 1), self.swap(block, 2)]

    def gather_far(self, first, second):
        half = first.shape[0] // 2
        return [self.swap(second[:half], 1), self.swap(first[half:], 2)]

    def sum_far(self, far_top, far_bottom):
        return [self.swap(far_top, 1), self.swap(far_bottom, 2)]

    def ring_start(self, sums, rows):
        level, _ = self.place()
        return lax.dynamic_slice_in_dim(sums, (level - 1) % self.planes * rows, rows, 0)

    def ring_step(self, total, sums, rows, step):
        level, _ = self.place()
        spot = (level - 1 - step) % self.planes * rows
        return wide(self.turn(low(total))) + lax.dynamic_slice_in_dim(sums, spot, rows, 0)

    def corners(self, part):
        rows, columns = part.shape[0] // self.devices, part.shape[1]
        parts = part.reshape(self.planes, PLANE, rows, columns)
        return pick_halves(parts, self.corner_spots())

    def sum_top(self, one_top, two_low):
        return [self.swap(one_top, 1), self.swap(two_low, 2)]

    def sum_low(self, one_low, two_top, far_one, far_two, waits=()):
        one, two = add_pairs([one_low, two_top], [far_two, far_one], waits)
        return [self.swap(one, 1), self.swap(two, 2)]

    def place_rows(self, rows, columns, bundles):
        level, corner = self.place()
        blocks, spots = [], []
        for start, parts in bundles:
            for other, lists in enumerate(parts):
                step = start
                for block in lists:
                    here = block.shape[0] // rows
                    for _ in range(here):
                        spots.append(((level - step) % self.planes) * PLANE + (corner ^ other))
                        step += 1
                    blocks.append(block.reshape(here, rows, columns))
        (whole,) = move(blocks, jnp.stack(spots))
        return whole.reshape(-1, columns)

    def cut_units(self, weights):
        core = lax.axis_index("tensor")
        rows, columns = weights[0].shape
        wanted = columns // 2
        pieces = jnp.stack(
            [
                jnp.concatenate(
                    [low(weight[:, half * wanted : (half + 1) * wanted]) for weight in weights],
                    axis=1,
                )
                for half in range(2)
            ],
            axis=0,
        ).reshape(2, 2, rows // 2, wanted * len(weights))
        keep = lax.dynamic_index_in_dim(pieces, core, 1, False)
        give = lax.dynamic_index_in_dim(pieces, 1 - core, 1, False)
        return keep, give

    def spread_units(self, keep, given):
        _, corner = self.place()
        quarters = order_cores(keep, given)
        arrived = []
        for other in range(PLANE):
            piece = lax.dynamic_slice_in_dim(quarters, corner ^ other, 1, 0)
            arrived.append(self.swap(piece, other) if other else piece)
        return arrived

    def place_plane(self, arrived, waits=()):
        return move(arrived, self.corner_spots(), None, waits)

    def gather_planes(self, plane):
        return lax.all_gather(plane, "dp", axis=0, tiled=True, axis_index_groups=self.columns)

    def place_units(self, own, other, cuts):
        core = lax.axis_index("tensor").astype(jnp.int32)
        parts = spread_halves(own, other, jnp.stack([core, 1 - core]), cuts)
        return [part.reshape(-1, part.shape[3]) for part in parts]

    def sum_planes(self, sums):
        return lax.psum_scatter(
            sums, "dp", scatter_dimension=0, tiled=True, axis_index_groups=self.columns
        )

    def return_units(self, total, waits=()):
        pieces = pick(total[None], self.corner_spots(), waits)
        arrived = [pieces[0]] + [self.swap(pieces[other], other) for other in (1, 2, 3)]
        return self.place_plane(arrived)[0]

    def join_units(self, quarters, count):
        core = lax.axis_index("tensor")
        keep = lax.dynamic_slice_in_dim(quarters, 2 * core, 2, 0)
        give = lax.dynamic_slice_in_dim(quarters, 2 - 2 * core, 2, 0)
        halves = order_cores(keep, swap_cores(give), axis=1)
        width = quarters.shape[2] // count
        return [
            wide(
                jnp.concatenate(
                    [halves[half][:, at * width : (at + 1) * width] for half in range(2)], axis=1
                )
            )
            for at in range(count)
        ]

    def gather_gains(self, corners, shape):
        level, corner = self.place()
        count, width = shape
        found = jnp.stack(corners, axis=0).reshape(self.devices, count * width)
        origin = jnp.arange(self.devices, dtype=jnp.int32)
        spot = ((origin % PLANE) ^ corner) * self.planes + (level - origin // PLANE) % self.planes
        choose = (spot[:, None] == origin[None, :]).astype(LOW)
        whole = jnp.dot(choose, found, preferred_element_type=jnp.float32)
        return jnp.swapaxes(whole.reshape(self.devices, count, width), 0, 1).reshape(count, -1)

    def own_gains(self, whole):
        width = whole.shape[1] // self.devices
        return lax.dynamic_slice(whole, (0, lax.axis_index("dp") * width), (whole.shape[0], width))


def shards(
    links,
    tokens,
    cotangent,
    segments,
    query_weight,
    key_weight,
    value_weight,
    out_weight,
    gate_weight,
    up_weight,
    down_weight,
    norm_gains,
    query_moment,
    key_moment,
    value_moment,
    out_moment,
    gate_moment,
    up_moment,
    down_moment,
    gains_moment,
    query_square,
    key_square,
    value_square,
    out_square,
    gate_square,
    up_square,
    down_square,
    gains_square,
):
    core = lax.axis_index("tensor")
    rows = tokens.shape[0]
    weight_rows, query_cols = query_weight.shape
    key_cols = key_weight.shape[1]
    into_cols = query_cols + 2 * key_cols
    units = gate_weight.shape[1]
    steps = links.planes

    def rows_of(values, which):
        return lax.dynamic_slice_in_dim(values, which * rows, rows, 0)

    def place_tokens(*blocks):
        half, columns = rows // 2, blocks[0].shape[1]
        lots = [block.reshape(-1, half, columns) for block in blocks]
        count = sum(lot.shape[0] for lot in lots)
        (whole,) = move(lots, jnp.arange(count, dtype=jnp.int32))
        return whole.reshape(-1, columns)

    gains_low = low(norm_gains)
    into_weight = jnp.concatenate([low(query_weight), low(key_weight), low(value_weight)], axis=1)
    units_keep, units_give = links.cut_units([down_weight, gate_weight, up_weight])
    gain_slots = [gains_low] + [links.shift(gains_low, step) for step in range(1, steps)]
    slots = [into_weight, links.turn(into_weight)]
    units_given = swap_cores(units_give)
    gains_level = jnp.stack(gain_slots, axis=0)
    gains_level, units_given, slots[1] = fence([gains_level, units_given, slots[1]])

    gain_corners = [gains_level] + [links.swap(gains_level, other) for other in (1, 2, 3)]
    spread = links.spread_units(units_keep, units_given)
    for _ in range(2, steps):
        slots.append(links.turn(slots[-1]))
    values = fence([*spread[1:], slots[-1]])
    spread[1:], slots[-1] = values[:3], values[3]

    (units_plane,) = links.place_plane(spread)
    units_own = links.gather_planes(units_plane)
    out_slots = [low(out_weight)]
    for _ in range(1, steps):
        out_slots.append(links.turn(out_slots[-1]))

    group = max(1, steps // 2)
    into_one = jnp.concatenate(slots[:group], axis=0)
    into_two = jnp.concatenate(slots[group:], axis=0)
    near_one = links.gather_near(into_one)
    gain_all = links.gather_gains(gain_corners, norm_gains.shape)
    gain_one = gain_all[0]
    gain_two = gain_all[1]
    normed_one = norm(tokens, gain_one)
    normed_one_all = order_rows(normed_one, swap_cores(normed_one))
    segment = segments[0]
    cosine, sine = rope_tables(segment)
    near_one = fence(near_one, [normed_one_all, cosine, sine])
    far_one = links.gather_far(*near_one)
    near_two = links.gather_near(into_two)
    *far_one, near_a, near_b = fence([*far_one, *near_two])
    near_two = [near_a, near_b]
    far_two = fence(links.gather_far(*near_two))
    into_all = links.place_rows(
        weight_rows,
        into_cols,
        [
            (0, [[into_one], [near_one[0]], [near_one[1]], far_one]),
            (group, [[into_two], [near_two[0]], [near_two[1]], far_two]),
        ],
    )

    (out_bundle,) = fence([jnp.concatenate(out_slots, axis=0)], far_two)
    out_near = links.gather_near(out_bundle)
    into = project(normed_one_all, into_all, cosine, sine, query_cols + key_cols)
    attended_one, totals_one = attend(into, segment, query_cols, 0)
    out_near = fence(out_near, [attended_one])
    out_far = links.gather_far(*out_near)
    attended_two, totals_two = attend(into, segment, query_cols, 1, out_near)
    *out_far, cotangent_late = fence([*out_far, *hold([cotangent])], [attended_two])
    upstream_near = links.gather_near(cotangent_late)
    out_all = links.place_rows(
        weight_rows, query_cols, [(0, [[out_bundle], [out_near[0]], [out_near[1]], out_far])]
    )
    attended = jnp.concatenate([attended_one, attended_two], axis=1)
    attn_other = low(contract_cols(rows_of(attended, 1 - core), out_all))
    attn_own = contract_cols(rows_of(attended, core), out_all)
    hidden_state = wide(tokens) + (attn_own + wide(swap_cores(attn_other)))
    normed_two = norm(hidden_state, gain_two)

    normed_near = links.gather_near(normed_two)
    upstream_near = fence(upstream_near, [normed_two])
    (units_own,) = fence([units_own], upstream_near)
    units_other = swap_cores(units_own)
    *normed_near, units_other = fence([*normed_near, units_other])
    normed_far = links.gather_far(*normed_near)
    down_all, gate_up_all = links.place_units(units_own, units_other, [units // 2])
    normed_front = place_tokens(normed_two, *normed_near)
    gate_up_front = gate_and_up(normed_front, gate_up_all)
    normed_far = fence(normed_far, [gate_up_front[:16, :LANES]])
    normed_back = place_tokens(*normed_far)

    upstream_near = fence(upstream_near, normed_far)
    upstream_far = links.gather_far(*upstream_near)
    gate_up_back = gate_and_up(normed_back, gate_up_all)
    upstream_front = place_tokens(cotangent_late, *upstream_near)
    inner_front, grads_front = hidden(upstream_front, down_all, gate_up_front)
    upstream_far = fence(upstream_far, [inner_front[:16, :LANES]])
    upstream_back = place_tokens(*upstream_far)
    inner_back, grads_back = hidden(upstream_back, down_all, gate_up_back)
    half = rows // 2
    back_far = across(grads_back, gate_up_all, 0, (half, half))
    back_far_sent = links.sum_far(*back_far)
    back_own, back_one, back_two = across(
        grads_front, gate_up_all, 0, (rows, rows, rows), [back_far[0]]
    )
    one_send, two_send = join_sends(back_one, back_two, *back_far_sent, [back_own])
    back_sent = [links.swap(one_send, 1), links.swap(two_send, 2)]
    down_keep, down_give, gate_up_keep, gate_up_give = unit_grads(
        [upstream_front, upstream_back],
        [inner_front, inner_back],
        [normed_front, normed_back],
        [grads_front, grads_back],
        weight_rows // 2,
        [one_send, two_send],
    )
    hidden_grad, attn_grad_low, gain_two_grad = norm_back(
        [back_own, *back_sent], hidden_state, gain_two, cotangent, [down_keep]
    )
    attn_grad_other = swap_cores(attn_grad_low)
    down_other = swap_cores(down_give)
    gate_up_other = swap_cores(gate_up_give)
    ffn_far = across(inner_back, down_all, 0, (half, half), [attn_grad_low])
    ffn_own, one_top, one_low, two_top, two_low = across(
        inner_front, down_all, 0, (rows, *[half] * 4), [attn_grad_low]
    )
    ffn_far_sent = links.sum_far(*ffn_far)
    ffn_near = [links.swap(one_top, 1), links.swap(two_low, 2)]
    unit_sums = add_low([(down_keep, down_other), (gate_up_keep, gate_up_other)], [ffn_own])
    units_sum = links.sum_planes(unit_sums)

    attn_grad_all = order_rows(attn_grad_low, attn_grad_other)
    attended_grad = plain(attn_grad_all, out_all, [ffn_own])
    out_own, one_top, one_low_out, two_top_out, two_low_out, *out_far = links.corners(
        inner_rows(attn_grad_all, attended, [attended_grad, unit_sums])
    )
    out_far_sent = links.sum_far(*out_far)
    out_top = links.sum_top(one_top, two_low_out)
    nothing = jnp.zeros((2 * rows, 2 * LANES), LOW)
    query_back_one, rest_back = attend_back(
        into,
        attended_grad,
        totals_one,
        cosine,
        sine,
        segment,
        nothing,
        0,
        [*ffn_far_sent, *ffn_near, *out_far],
    )
    out_low = links.sum_low(one_low_out, two_top_out, *out_far_sent, [rest_back])
    query_back_two, rest_back = attend_back(
        into, attended_grad, totals_two, cosine, sine, segment, rest_back, 1, out_top
    )
    into_back = jnp.concatenate([query_back_one, query_back_two, rest_back], axis=1)
    into_own, into_one_top, into_one_low, into_two_top, into_two_low, *into_far = links.corners(
        inner_rows(normed_one_all, into_back, out_low)
    )
    into_far_sent = links.sum_far(*into_far)
    into_top = links.sum_top(into_one_top, into_two_low)
    out_sent = [
        jnp.concatenate([out_top[0], out_low[0]], axis=0),
        jnp.concatenate([out_low[1], out_top[1]], axis=0),
    ]
    (normed_part,) = across(into_back, into_all, 0, (2 * rows,), into_far)
    out_sums = wide(out_own) + wide(out_sent[0]) + wide(out_sent[1])
    out_shard = links.ring_start(out_sums, weight_rows)
    out_shard = links.ring_step(out_shard, out_sums, weight_rows, 1)
    into_low = links.sum_low(
        into_one_low, into_two_top, *into_far_sent, [normed_part, *into_top]
    )
    normed_own, normed_other = part_rows(normed_part, into_far_sent)
    input_grad, _, gain_one_grad = norm_back(
        [normed_own, swap_cores(normed_other)], tokens, gain_one, hidden_grad
    )
    gains_part = jnp.concatenate([gain_one_grad, gain_two_grad], axis=0)
    gains_part = gains_part + swap_cores(gains_part)
    for step in range(2, steps):
        out_shard = links.ring_step(out_shard, out_sums, weight_rows, step)
    into_low = hold(into_low, [gains_part])
    into_sent = [
        jnp.concatenate([into_top[0], into_low[0]], axis=0),
        jnp.concatenate([into_low[1], into_top[1]], axis=0),
    ]
    into_sums = wide(into_own) + wide(into_sent[0]) + wide(into_sent[1])
    into_shard = links.ring_start(into_sums, weight_rows)
    into_shard = links.ring_step(into_shard, into_sums, weight_rows, 1)
    (gains_part,) = hold([gains_part], into_low)
    gains_level = gains_part
    for block in [links.shift(gains_part, step) for step in range(1, steps)]:
        gains_level = gains_level + block
    one_send, two_send = hold(
        [low(wide(one_low) + wide(ffn_far_sent[1])), low(wide(two_top) + wide(ffn_far_sent[0]))],
        into_low,
    )
    ffn_low = [links.swap(one_send, 1), links.swap(two_send, 2)]
    units_back = links.return_units(units_sum, ffn_low)
    for step in range(2, steps):
        if step == steps - 1:
            (into_shard,) = hold([into_shard], [gains_level, *ffn_low])
        into_shard = links.ring_step(into_shard, into_sums, weight_rows, step)
    gains_others = [links.swap(gains_level, other) for other in (1, 2, 3)]
    gains_shard = links.own_gains(gains_level + gains_others[0] + gains_others[1] + gains_others[2])
    down_shard, gate_shard, up_shard = links.join_units(units_back, 3)
    ffn_sum = jnp.concatenate(
        [
            wide(ffn_near[0]) + wide(ffn_low[1]),
            wide(ffn_low[0]) + wide(ffn_near[1]),
        ],
        axis=0,
    )
    activations = low(hidden_state + (wide(ffn_own) + ffn_sum))
    query_shard = into_shard[:, :query_cols]
    key_shard = into_shard[:, query_cols : query_cols + key_cols]
    value_shard = into_shard[:, query_cols + key_cols :]
    q_all = adam(query_weight, query_shard, query_moment, query_square, RATE_MAIN, DECAY_RATE)
    k_all = adam(key_weight, key_shard, key_moment, key_square, RATE_MAIN, DECAY_RATE)
    v_all = adam(value_weight, value_shard, value_moment, value_square, RATE_MAIN, DECAY_RATE)
    o_all = adam(out_weight, out_shard, out_moment, out_square, RATE_OUT, DECAY_RATE)
    g_all = adam(gate_weight, gate_shard, gate_moment, gate_square, RATE_MAIN, DECAY_RATE)
    u_all = adam(up_weight, up_shard, up_moment, up_square, RATE_MAIN, DECAY_RATE)
    d_all = adam(down_weight, down_shard, down_moment, down_square, RATE_DOWN, DECAY_RATE)
    n_all = adam(norm_gains, gains_shard, gains_moment, gains_square, RATE_GAINS, 0.0)
    return (
        activations,
        input_grad,
        q_all[0],
        q_all[1],
        q_all[2],
        q_all[3],
        k_all[0],
        k_all[1],
        k_all[2],
        k_all[3],
        v_all[0],
        v_all[1],
        v_all[2],
        v_all[3],
        o_all[0],
        o_all[1],
        o_all[2],
        o_all[3],
        g_all[0],
        g_all[1],
        g_all[2],
        g_all[3],
        u_all[0],
        u_all[1],
        u_all[2],
        u_all[3],
        d_all[0],
        d_all[1],
        d_all[2],
        d_all[3],
        n_all[0],
        n_all[1],
        n_all[2],
        n_all[3],
    )


def solution(mesh):
    in_specs = (
        P(("dp", "tensor"), None),
        P(("dp", "tensor"), None),
        P("dp", None),
        P("dp", "tensor"),
        P("dp", "tensor"),
        P("dp", "tensor"),
        P("dp", "tensor"),
        P("dp", "tensor"),
        P("dp", "tensor"),
        P("dp", "tensor"),
        P(None, "dp"),
        P("dp", "tensor"),
        P("dp", "tensor"),
        P("dp", "tensor"),
        P("dp", "tensor"),
        P("dp", "tensor"),
        P("dp", "tensor"),
        P("dp", "tensor"),
        P(None, "dp"),
        P("dp", "tensor"),
        P("dp", "tensor"),
        P("dp", "tensor"),
        P("dp", "tensor"),
        P("dp", "tensor"),
        P("dp", "tensor"),
        P("dp", "tensor"),
        P(None, "dp"),
    )
    out_specs = (
        P(("dp", "tensor"), None),
        P(("dp", "tensor"), None),
        P("dp", "tensor"),
        P("dp", "tensor"),
        P("dp", "tensor"),
        P("dp", "tensor"),
        P("dp", "tensor"),
        P("dp", "tensor"),
        P("dp", "tensor"),
        P("dp", "tensor"),
        P("dp", "tensor"),
        P("dp", "tensor"),
        P("dp", "tensor"),
        P("dp", "tensor"),
        P("dp", "tensor"),
        P("dp", "tensor"),
        P("dp", "tensor"),
        P("dp", "tensor"),
        P("dp", "tensor"),
        P("dp", "tensor"),
        P("dp", "tensor"),
        P("dp", "tensor"),
        P("dp", "tensor"),
        P("dp", "tensor"),
        P("dp", "tensor"),
        P("dp", "tensor"),
        P("dp", "tensor"),
        P("dp", "tensor"),
        P("dp", "tensor"),
        P("dp", "tensor"),
        P(None, "dp"),
        P(None, "dp"),
        P(None, "dp"),
        P(None, "dp"),
    )
    links = Links(mesh.shape["dp"])
    return jax.shard_map(functools.partial(shards, links), mesh=mesh, in_specs=in_specs, out_specs=out_specs, check_vma=False)
```
